256 devices in a mesh: sx: 8 (over y_lo, x), sy: 16 (over z, core), hd: 2 (over y_hi).
Axes of the slice: x: 4, y: 4 (y_hi: 2, y_lo: 2; y = y_hi * 2 + y_lo), z: 8, core: 2. Of those that a mesh axis runs over, the one named last changes fastest.
Arguments:
- queries: bfloat16 [16, 32, 12, 32, 128], P('sx', 'sy', 'hd'), may hold values from -10 to 10
- key_field: bfloat16 [16, 32, 12, 32, 128], P('sx', 'sy', 'hd'), may hold values from -10 to 10
- value_field: bfloat16 [16, 32, 12, 32, 128], P('sx', 'sy', 'hd'), may hold values from -6 to 6
- grad_output: bfloat16 [16, 32, 384, 128], P('sx', 'sy'), may hold values from -6 to 6
- out_weight: bfloat16 [384, 384], P('hd'), may hold values from -0.3125 to 0.3125
- window_counts: int32 [16, 32], P('sx', 'sy'), may hold values from 1 to 8
- adjacent: int32 [16, 32, 2], P('sx', 'sy'), may hold values from 0 to 3, all different within a row
- far_list: int32 [16, 32, 4], P('sx', 'sy'), may hold values from 0 to 15, all different within a row
Outputs:
- block_out: bfloat16 [16, 32, 384, 128], P('sx', 'sy', 'hd')
- grad_queries: bfloat16 [16, 32, 12, 32, 128], P('sx', 'sy', 'hd')
- grad_key_field: bfloat16 [16, 32, 12, 32, 128], P('sx', 'sy', 'hd')
- grad_value_field: bfloat16 [16, 32, 12, 32, 128], P('sx', 'sy', 'hd')
The draws below stay inside these ranges and needn't reach their ends.
Inputs may be any that keep to these rules, and one draw needn't show every extreme that they name: `adjacent`: the codes of one window are distinct. `far_list`: entry e names coarse row e // 16 of the 1 coarse rows covering the window's block of 2 window rows, coarse column e % 16; the entries of one window are distinct.
All inputs are finite; a program needn't handle non-finite values.
Results may differ from the reference program's by a relative error of at most 0.012.
Values may be sent and summed in bfloat16 or wider, within the bound.
A program may use at most 128 MiB of HBM per device.

```python
import math
import jax
import jax.numpy as jnp
from jax import lax

HEADS = 12
DH = 32
C = 384
WIN = 128
PGRP = 16
GROUPS = 8
NADJ = 2
NFAR = 4
WD = 2
NWX = 16
NWY = 32
NCY = 16
STRIP = 16


def draw_queries(key, part):
    key = jax.random.fold_in(key, 11)
    shape = (NWX, NWY, HEADS, DH, WIN)
    drawn = jnp.clip(jax.random.normal(key, shape, jnp.float32), -4.0, 4.0)
    return drawn.astype(jnp.bfloat16)


def draw_key_field(key, part):
    key = jax.random.fold_in(key, 23)
    shape = (NWX, NWY, HEADS, DH, WIN)
    drawn = jnp.clip(jax.random.normal(key, shape, jnp.float32), -4.0, 4.0)
    return drawn.astype(jnp.bfloat16)


def place_ends(array, own_key, smallest, top_value):
    spot = [jax.random.randint(jax.random.fold_in(own_key, axis), (), 0, length) for axis, length in enumerate(array.shape)]
    widest = array.shape.index(max(array.shape))
    next_to = spot[:widest] + [(spot[widest] + 1) % array.shape[widest]] + spot[widest + 1:]
    return array.at[tuple(spot)].set(smallest).at[tuple(next_to)].set(top_value)


def block_levels(own_key, shape, pieces, low, high):
    factor_of, own = 1.0, jax.random.fold_in(own_key, 6)
    for dim, parts in pieces:
        draws = jnp.exp(jax.random.uniform(jax.random.fold_in(own, dim), (parts,), jnp.float32, low / len(pieces), high / len(pieces)))
        factor_of = factor_of * jnp.repeat(draws, shape[dim] // parts).reshape([-1 if axis == dim else 1 for axis in range(len(shape))])
    return factor_of


def different_ones(rng, rows, amount, top, lift):
    ranking = jax.random.permutation(jax.random.fold_in(rng, 1), amount)
    boost = ranking
    for power in range(3):
        boost = boost * boost // amount
    boost = boost * lift // amount
    lots = jax.random.randint(jax.random.fold_in(rng, 2), (rows, amount), 0, 4096) + boost
    sure = jax.random.permutation(jax.random.fold_in(rng, 3), rows)[jnp.arange(amount) % rows]
    lots = jnp.where(jnp.arange(rows)[:, None] == sure[None, :], 1 << 14, lots)
    priority = lots * amount + jnp.arange(amount)
    return lax.top_k(priority.astype(jnp.int32), top)[1].astype(jnp.int32)


def gaussian(key, dims, width, bound, pieces=(), kind=jnp.bfloat16):
    values = width * jax.random.normal(key, dims, jnp.float32)
    if pieces:
        values = values * block_levels(key, dims, pieces, -0.22, 0.18)
    return jnp.clip(values, -bound, bound).astype(kind)


def setup_inputs(seed: int = 0) -> dict:
    arg_keys = jax.random.split(jax.random.key(seed), 9)
    return {
        "queries": draw_queries(jax.random.fold_in(arg_keys[8], 71), 0),
        "key_field": draw_key_field(jax.random.fold_in(arg_keys[8], 71), 0),
        "value_field": gaussian(arg_keys[2], (NWX, NWY, HEADS, DH, WIN), 1.0, 6.0, ((0, 8), (1, 16), (2, 2))),
        "grad_output": gaussian(arg_keys[3], (NWX, NWY, C, WIN), 1.0, 6.0, ((0, 8), (1, 16))),
        "out_weight": gaussian(arg_keys[4], (C, C), C ** -0.5, 0.3125, ((0, 2),)),
        "window_counts": place_ends(jax.random.randint(arg_keys[5], (NWX, NWY), 1, GROUPS + 1), jax.random.fold_in(arg_keys[5], 1), 1, GROUPS).astype(jnp.int32),
        "adjacent": different_ones(arg_keys[6], NWX * NWY, 4, NADJ, 0).reshape((NWX, NWY, NADJ)),
        "far_list": different_ones(arg_keys[7], NWX * NWY, STRIP, NFAR, 0).reshape((NWX, NWY, NFAR)),
    }


def pool_pairs(stacked, group_size):
    grid_x, grid_y, pair_dim, head_count, head_dim, window_len = stacked.shape
    cell_count = window_len // group_size
    grouped = stacked.astype(jnp.float32).reshape(grid_x // 2, 2, grid_y // 2, 2, pair_dim, head_count, head_dim, cell_count, group_size)
    pooled = lax.optimization_barrier(jnp.mean(grouped, axis=8))
    pooled = jnp.transpose(pooled, (0, 2, 4, 5, 6, 1, 3, 7))
    return pooled.reshape(grid_x // 2, grid_y // 2, pair_dim, head_count, head_dim, 4 * cell_count).astype(jnp.bfloat16)

def pooled_valid(window_counts, cell_count):
    grid_x, grid_y = window_counts.shape
    quarter_counts = jnp.transpose(window_counts.reshape(grid_x // 2, 2, grid_y // 2, 2), (0, 2, 1, 3)).reshape(grid_x // 2, grid_y // 2, 4)
    is_valid = jnp.arange(cell_count, dtype=jnp.int32)[None, None, None, :] < quarter_counts[:, :, :, None]
    return is_valid.reshape(grid_x // 2, grid_y // 2, 4 * cell_count).astype(jnp.int32)

def spread_pooled(grads_in, group_size):
    half_x, half_y, pair_dim, head_count, head_dim, pooled_len = grads_in.shape
    cell_count = pooled_len // 4
    split = grads_in.reshape(half_x, half_y, pair_dim, head_count, head_dim, 2, 2, cell_count)
    split = jnp.transpose(split, (0, 5, 1, 6, 2, 3, 4, 7)).reshape(2 * half_x, 2 * half_y, pair_dim, head_count, head_dim, cell_count)
    spread = jnp.broadcast_to(split[..., None], split.shape + (group_size,))
    return spread.reshape(split.shape[:5] + (cell_count * group_size,)) / group_size

def direction_steps(adjacent_row):
    step_x = (adjacent_row == 1).astype(jnp.int32) - (adjacent_row == 0).astype(jnp.int32)
    step_y = (adjacent_row == 3).astype(jnp.int32) - (adjacent_row == 2).astype(jnp.int32)
    return (step_x, step_y)

def assemble(own_part, beside, far_part, own_count, beside_count, far_mask, group_size):
    blocks, slot_count = (beside.shape[0], beside.shape[1])
    pair_dim, head_count, head_dim, window_len = (own_part.shape[1], own_part.shape[2], own_part.shape[3], own_part.shape[4])
    beside_flat = jnp.transpose(beside, (0, 2, 3, 4, 1, 5)).reshape(blocks, pair_dim, head_count, head_dim, -1)
    far_flat = jnp.transpose(far_part, (0, 2, 3, 4, 1, 5)).reshape(blocks, pair_dim, head_count, head_dim, -1)
    joined = jnp.concatenate([own_part, beside_flat, far_flat], axis=4)
    positions = jnp.arange(window_len, dtype=jnp.int32)
    own_valid = positions[None, :] < group_size * own_count[:, None]
    beside_valid = (positions[None, None, :] < group_size * beside_count[:, :, None]).reshape(blocks, -1)
    far_valid = (far_mask > 0).reshape(blocks, -1)
    key_mask = jnp.concatenate([own_valid, beside_valid, far_valid], axis=1)
    return (joined[:, 0], joined[:, 1], key_mask)

def split_grads(grad_keys, grad_values, window_len, slot_count, far_count):
    blocks, head_count, head_dim = (grad_keys.shape[0], grad_keys.shape[1], grad_keys.shape[2])
    paired = jnp.stack([grad_keys, grad_values], axis=1)
    own_grad = paired[..., :window_len]
    near_end = window_len * (1 + slot_count)
    beside_grad = paired[..., window_len:near_end].reshape(blocks, 2, head_count, head_dim, slot_count, window_len)
    beside_grad = jnp.transpose(beside_grad, (0, 4, 1, 2, 3, 5))
    far_grad = paired[..., near_end:].reshape(blocks, 2, head_count, head_dim, far_count, -1)
    far_grad = jnp.transpose(far_grad, (0, 4, 1, 2, 3, 5))
    return (own_grad, beside_grad, far_grad)

def window_pass(query_rows, grad_rows, key_block, value_block, key_mask, query_mask):
    score_scale = 1.0 / math.sqrt(query_rows.shape[2])
    query_wide = query_rows.astype(jnp.float32)
    grad_wide = grad_rows.astype(jnp.float32)
    key_wide = key_block.astype(jnp.float32)
    value_wide = value_block.astype(jnp.float32)
    scores = jnp.einsum('bhdi,bhdj->bhij', query_wide, key_wide) * score_scale
    scores = jnp.where(key_mask[:, None, None, :], scores, -jnp.inf)
    row_max = lax.optimization_barrier(jnp.max(scores, axis=3, keepdims=True))
    exponent = jnp.exp(scores - row_max)
    weights = exponent / lax.optimization_barrier(jnp.sum(exponent, axis=3, keepdims=True))
    weights_low = weights.astype(jnp.bfloat16)
    low_wide = weights_low.astype(jnp.float32)
    attended = jnp.einsum('bhij,bhdj->bhdi', low_wide, value_wide)
    attended = jnp.where(query_mask[:, None, None, :], attended, 0.0).astype(jnp.bfloat16)
    grad_prob = jnp.einsum('bhdi,bhdj->bhij', grad_wide, value_wide)
    centre = lax.optimization_barrier(jnp.sum(weights * grad_prob, axis=3, keepdims=True))
    grad_score = (weights * (grad_prob - centre) * score_scale).astype(jnp.bfloat16)
    score_wide = grad_score.astype(jnp.float32)
    grad_query = jnp.einsum('bhij,bhdj->bhdi', score_wide, key_wide)
    grad_keys = jnp.einsum('bhij,bhdi->bhdj', score_wide, query_wide)
    grad_values = jnp.einsum('bhij,bhdi->bhdj', low_wide, grad_wide)
    return (attended, grad_query, grad_keys, grad_values)

def reference(queries, key_field, value_field, grad_output, out_weight, window_counts, adjacent, far_list):
    grid_x, grid_y, head_count, head_dim, window_len = queries.shape
    cell_count = window_len // PGRP
    stacked = jnp.stack([key_field, value_field], axis=2)
    pooled = pool_pairs(stacked, PGRP)
    pooled_mask = pooled_valid(window_counts, cell_count)
    stacked_pad = jnp.pad(stacked, ((1, 1), (1, 1), (0, 0), (0, 0), (0, 0), (0, 0)))
    counts_pad = jnp.pad(window_counts, 1)
    positions = jnp.arange(window_len, dtype=jnp.int32)
    query_valid = positions[None, None, :] < PGRP * window_counts[:, :, None]
    grad_mixed = jnp.einsum('fc,abci->abfi', out_weight.astype(jnp.float32), grad_output.astype(jnp.float32))
    grad_mixed = jnp.where(query_valid[:, :, None, :], grad_mixed, 0.0).astype(jnp.bfloat16)
    grad_mixed = grad_mixed.reshape(queries.shape)
    columns = jnp.arange(grid_y, dtype=jnp.int32)

    def row_step(state_in, inputs):
        previous, current, coarse_grads = state_in
        row_index, query_row, grad_row, adjacent_row, far_row, count_row = inputs
        step_x, step_y = direction_steps(adjacent_row)
        near_x = row_index + 1 + step_x
        near_y = columns[:, None] + 1 + step_y
        own_part = lax.dynamic_index_in_dim(stacked_pad, row_index + 1, 0, keepdims=False)[1:grid_y + 1]
        beside = stacked_pad[near_x, near_y]
        beside_count = counts_pad[near_x, near_y]
        strip_base = row_index // WD * (WD // 2)
        far_x = strip_base + far_row // NCY
        far_y = far_row % NCY
        far_part = pooled[far_x, far_y]
        far_mask = pooled_mask[far_x, far_y]
        key_block, value_block, key_mask = assemble(own_part, beside, far_part, count_row, beside_count, far_mask, PGRP)
        query_mask = positions[None, :] < PGRP * count_row[:, None]
        attended, grad_query, grad_keys, grad_values = window_pass(query_row, grad_row, key_block, value_block, key_mask, query_mask)
        own_grad, beside_grad, far_grad = split_grads(grad_keys, grad_values, window_len, beside.shape[1], far_row.shape[1])
        row_band = jnp.zeros((3, grid_y + 2) + own_grad.shape[1:], jnp.float32)
        row_band = row_band.at[1, 1:grid_y + 1].add(own_grad)
        row_band = row_band.at[1 + step_x, near_y].add(beside_grad)
        coarse_grads = coarse_grads.at[far_x, far_y].add(far_grad)
        finished = previous + row_band[0]
        return ((current + row_band[1], row_band[2], coarse_grads), (finished, attended, grad_query.astype(jnp.bfloat16)))
    band_shape = (grid_y + 2,) + stacked.shape[2:]
    start_state = (jnp.zeros(band_shape, jnp.float32), jnp.zeros(band_shape, jnp.float32), jnp.zeros(pooled.shape, jnp.float32))
    row_inputs = (jnp.arange(grid_x, dtype=jnp.int32), queries, grad_mixed, adjacent, far_list, window_counts)
    (previous, current, coarse_grads), (finished, attended, grad_queries) = lax.scan(row_step, start_state, row_inputs)
    near_rows = jnp.concatenate([finished[1:], previous[None]], axis=0)[:, 1:grid_y + 1]
    totals = near_rows + spread_pooled(coarse_grads, PGRP)
    flat_out = attended.reshape(grid_x, grid_y, head_count * head_dim, window_len)
    block_out = jnp.einsum('abfi,fc->abci', flat_out.astype(jnp.float32), out_weight.astype(jnp.float32)).astype(jnp.bfloat16)
    return (block_out, grad_queries, totals[:, :, 0].astype(jnp.bfloat16), totals[:, :, 1].astype(jnp.bfloat16))
```

```python
import math

import jax
import jax.numpy as jnp
from jax import lax
from jax.experimental import pallas as pl
from jax.experimental.pallas import tpu as pltpu
from jax.sharding import PartitionSpec as P

MESH = pl.DeviceIdType.MESH
BF, F32 = jnp.bfloat16, jnp.float32
WIN = 128
DH = 32
FEAT = 192
AUG = 208
BLK = AUG + FEAT
PAIRS = 3
GRP = 16
MASKED = -1e30
MARK = 1e4
SCALE = 1.0 / math.sqrt(DH)
EXPC = SCALE * math.log2(math.e)
PARTS = ((0, 1), (1, 3), (3, 4))
NT = (((1,), (1,)), ((), ()))


def dot(a, b):
    return jnp.dot(a, b, preferred_element_type=F32)


def dot_nt(a, b):
    return lax.dot_general(a, b, NT, preferred_element_type=F32)


def iota(shape, dim):
    return lax.broadcasted_iota(jnp.int32, shape, dim)


def diagonal(first, second):
    zero = jnp.zeros_like(first)
    return jnp.concatenate(
        [jnp.concatenate([first, zero], 1), jnp.concatenate([zero, second], 1)], 0
    )


def placed(pair, p, tail):
    pieces = [pair]
    if p > 0:
        pieces = [jnp.zeros((64 * p, 256), BF)] + pieces
    if p < PAIRS - 1:
        pieces = pieces + [jnp.zeros((64 * (PAIRS - 1 - p), 256), BF)]
    return jnp.concatenate(pieces + [tail, jnp.zeros((48, 256), BF)], 0)


def neighbours(w):
    r, c = divmod(w, 2)
    return (
        w - 2 if r else 4 + c,
        6 + c if r else w + 2,
        w - 1 if c else 8 + r,
        10 + r if c else w + 1,
    )


def kernel(
    n_x,
    n_y,
    q_ref,
    k_ref,
    v_ref,
    go_ref,
    ow_ref,
    cnt_ref,
    adj_ref,
    far_ref,
    bo_ref,
    gq_ref,
    gk_ref,
    gv_ref,
    kvx,
    keys,
    kt,
    vt,
    pool,
    gm,
    owt,
    e_s,
    m_s,
    a_s,
    f_s,
    c_s,
    att,
    gq_s,
    g_s,
    pg_out,
    pg_in,
    rim_out,
    rim_in,
    bo_out,
    bo_in,
    bo_own,
    halo_send,
    halo_recv,
    pool_send,
    pool_recv,
    rim_send,
    rim_recv,
    pg_send,
    pg_recv,
    bo_send,
    bo_recv,
):
    sx, sy, hd = lax.axis_index("sx"), lax.axis_index("sy"), lax.axis_index("hd")
    up, down = sx > 0, sx < n_x - 1
    left, right = sy > 0, sy < n_y - 1
    x_lo, x_hi = {"sx": jnp.maximum(sx - 1, 0)}, {"sx": jnp.minimum(sx + 1, n_x - 1)}
    y_lo, y_hi = {"sy": jnp.maximum(sy - 1, 0)}, {"sy": jnp.minimum(sy + 1, n_y - 1)}
    peers = [lax.rem(sy + off, n_y) for off in range(1, n_y)]

    barrier = pltpu.get_barrier_semaphore()

    def greet(where):
        pl.semaphore_signal(barrier, inc=1, device_id=where, device_id_type=MESH)

    pl.when(up)(lambda: greet(x_lo))
    pl.when(down)(lambda: greet(x_hi))
    greet({"hd": 1 - hd})
    for peer in peers:
        greet({"sy": peer})

    pooled = None
    for w in range(4):
        r, c = divmod(w, 2)
        keep = GRP * cnt_ref[r, c]
        off = (iota((16, WIN), 0) == 0) & (iota((16, WIN), 1) >= keep)
        mask = jnp.where(off, MASKED, 0.0).astype(BF)
        block = jnp.concatenate([k_ref[w], mask, v_ref[w]], 0)
        kvx[w] = block
        keys[w, 0] = block
        row, lane = iota((32, WIN), 0), iota((32, WIN), 1)
        member = jnp.where(row == 8 * w + lane // GRP, 1.0, 0.0).astype(BF)
        part = dot_nt(member, jnp.concatenate([k_ref[w], v_ref[w]], 0))
        row, lane = iota((32, 2 * FEAT), 0), iota((32, 2 * FEAT), 1)
        bad = (lane == 0) & (row >= 8 * w + cnt_ref[r, c]) & (row < 8 * w + 8)
        part = jnp.where(bad, MARK, part * (1.0 / GRP))
        pooled = part if pooled is None else pooled + part
    pool[sy] = pooled.astype(BF)

    pl.semaphore_wait(barrier, n_y + up.astype(jnp.int32) + down.astype(jnp.int32))

    def remote(src, dst, sends, recvs, i, j, where):
        return pltpu.make_async_remote_copy(
            src_ref=src,
            dst_ref=dst,
            send_sem=sends.at[i],
            recv_sem=recvs.at[j],
            device_id=where,
            device_id_type=MESH,
        )

    def halo(src, dst, i, where):
        return remote(kvx.at[src], kvx.at[dst], halo_send, halo_recv, i, i, where)

    halos = (
        (up, [halo(pl.ds(0, 2), pl.ds(6, 2), 0, x_lo)]),
        (down, [halo(pl.ds(2, 2), pl.ds(4, 2), 1, x_hi)]),
        (left, [halo(0, 10, 2, y_lo), halo(2, 11, 3, y_lo)]),
        (right, [halo(1, 8, 4, y_hi), halo(3, 9, 5, y_hi)]),
    )
    arrivals = ((up, [1], 4), (down, [0], 6), (left, [4, 5], 8), (right, [2, 3], 10))
    flat = [copy for _, copies in halos for copy in copies]

    def start_all(copies):
        for copy in copies:
            copy.start()

    def wait_sends(copies):
        for copy in copies:
            copy.wait_send()

    def wait_recvs(copies):
        for copy in copies:
            copy.wait_recv()

    pool_copies = [
        remote(pool.at[sy], pool.at[sy], pool_send, pool_recv, i, sy, {"sy": peer})
        for i, peer in enumerate(peers)
    ]
    pool_arrivals = [
        remote(pool.at[peer], pool.at[peer], pool_send, pool_recv, i, peer, {"sy": peer})
        for i, peer in enumerate(peers)
    ]
    for there, copies in halos:
        pl.when(there)(lambda copies=copies: start_all(copies))
    start_all(pool_copies)

    for w in range(4):
        r, c = divmod(w, 2)
        mixed = dot(ow_ref[...], go_ref[w])
        mixed = jnp.where(iota((FEAT, WIN), 1) < GRP * cnt_ref[r, c], mixed, 0.0)
        gm[w] = mixed.astype(BF)
    owt[...] = ow_ref[...].T

    def turn(w, b, block):
        pad = jnp.zeros((48, WIN), BF)
        kt[w, pl.ds(WIN * b, WIN), :] = jnp.concatenate([block[:AUG], pad], 0).T
        vt[w, pl.ds(WIN * b, WIN), :] = jnp.concatenate(
            [block[AUG:], jnp.zeros((64, WIN), BF)], 0
        ).T

    for w in range(4):
        turn(w, 0, keys[w, 0])

    def rows_of(w, part, base, p):
        first, last = PARTS[part]
        return jnp.concatenate(
            [keys[w, b, base + 64 * p : base + 64 * p + 64, :] for b in range(first, last)], 1
        )

    def forward(part):
        first, last = PARTS[part]
        lo, n = WIN * first, WIN * (last - first)
        one_row = jnp.where(iota((16, 256), 0) == 0, 1.0, 0.0).astype(BF)
        ones = jnp.ones((16, n), BF)

        def body(w, carry):
            for p in range(PAIRS):
                pair = diagonal(
                    q_ref[w, 64 * p : 64 * p + 32, :], q_ref[w, 64 * p + 32 : 64 * p + 64, :]
                )
                scores = dot(kt[w, lo : lo + n, :], placed(pair, p, one_row))
                top = jnp.max(scores, axis=0, keepdims=True)
                low = jnp.exp2((scores - top) * EXPC).astype(BF)
                e_s[w, p, lo : lo + n, :] = low
                rows = jnp.concatenate([rows_of(w, part, AUG, p), ones], 0)
                a_s[w, p, part] = dot(rows, low)
                m_s[w, p, part] = jnp.broadcast_to(top, (8, 256))
            return carry

        lax.fori_loop(0, 4, body, 0)

    forward(0)

    for there, index, slot in arrivals:

        def arrive(index=index):
            wait_recvs([flat[i] for i in index])

        def outside(slot=slot):
            off = iota((2, BLK, WIN), 1) == FEAT
            kvx[slot : slot + 2] = jnp.where(off, MASKED, 0.0).astype(BF)

        pl.when(there)(arrive)
        pl.when(jnp.logical_not(there))(outside)

    for w in range(4):
        r, c = divmod(w, 2)
        n0, n1, n2, n3 = neighbours(w)
        for s in range(2):
            code = adj_ref[r, c, s]
            slot = jnp.where(
                code < 2, jnp.where(code == 0, n0, n1), jnp.where(code == 2, n2, n3)
            )
            block = kvx[slot]
            keys[w, 1 + s] = block
            turn(w, 1 + s, block)

    forward(1)

    wait_recvs(pool_arrivals)
    for w in range(4):
        r, c = divmod(w, 2)
        listed = jnp.concatenate([pool[far_ref[r, c, f]] for f in range(4)], 0).T
        bad = (iota((16, WIN), 0) == 0) & (listed[:16].astype(F32) > 0.5 * MARK)
        mask = jnp.where(bad, MASKED, 0.0).astype(BF)
        block = jnp.concatenate([listed[:FEAT], mask, listed[FEAT:]], 0)
        keys[w, 3] = block
        turn(w, 3, block)

    forward(2)

    def combine(w, carry):
        keep = GRP * cnt_ref[w // 2, w % 2]
        for p in range(PAIRS):
            tops = [m_s[w, p, i, 0:1, :] for i in range(3)]
            top = jnp.maximum(jnp.maximum(tops[0], tops[1]), tops[2])
            shares = [jnp.exp2((t - top) * EXPC) for t in tops]
            total = sum(share * a_s[w, p, i] for i, share in enumerate(shares))
            inverse = 1.0 / total[64:65]
            first = total[:32, :WIN] * inverse[:, :WIN]
            second = total[32:64, WIN:] * inverse[:, WIN:]
            both = jnp.concatenate([first, second], 0)
            product = both * gm[w, 64 * p : 64 * p + 64, :].astype(F32)
            centre = jnp.concatenate(
                [
                    jnp.sum(product[:32], axis=0, keepdims=True),
                    jnp.sum(product[32:], axis=0, keepdims=True),
                ],
                1,
            )
            c_s[w, p] = jnp.broadcast_to(centre, (8, 256))
            for i, share in enumerate(shares):
                f_s[w, p, i] = jnp.broadcast_to(share * inverse, (8, 256))
            both = jnp.where(iota((64, WIN), 1) < keep, both, 0.0)
            att[w, 64 * p : 64 * p + 64, :] = both.astype(BF)
        return carry

    lax.fori_loop(0, 4, combine, 0)

    mine = pl.ds(pl.multiple_of(hd * FEAT, FEAT), FEAT)
    theirs = pl.ds(pl.multiple_of((1 - hd) * FEAT, FEAT), FEAT)
    for w in range(4):
        bo_out[w] = dot(owt[theirs, :], att[w]).astype(BF)
    bo_copy = remote(bo_out, bo_in, bo_send, bo_recv, 0, 0, {"hd": 1 - hd})
    bo_copy.start()

    def backward(part):
        first, last = PARTS[part]
        lo, n = WIN * first, WIN * (last - first)
        no_row = jnp.zeros((16, 256), BF)

        def body(w, carry):
            for p in range(PAIRS):
                one, two = slice(64 * p, 64 * p + 32), slice(64 * p + 32, 64 * p + 64)
                factor = f_s[w, p, part, 0:1, :]
                grad_one, grad_two = gm[w, one, :], gm[w, two, :]
                prob = dot(vt[w, lo : lo + n, :], placed(diagonal(grad_one, grad_two), p, no_row))
                low = e_s[w, p, lo : lo + n, :]
                slope = (low.astype(F32) * (prob - c_s[w, p, 0:1, :])).astype(BF)
                scaled = factor * SCALE
                back = dot(rows_of(w, part, 0, p), slope) * scaled
                back = jnp.concatenate([back[:32, :WIN], back[32:, WIN:]], 0)
                if part != 2:
                    back = back + gq_s[w, 64 * p : 64 * p + 64, :]
                if part == 0:
                    gq_ref[w, 64 * p : 64 * p + 64, :] = back.astype(BF)
                else:
                    gq_s[w, 64 * p : 64 * p + 64, :] = back
                rows = diagonal(
                    (q_ref[w, one, :].astype(F32) * scaled[:, :WIN]).astype(BF),
                    (q_ref[w, two, :].astype(F32) * scaled[:, WIN:]).astype(BF),
                )
                g_s[w, 64 * p : 64 * p + 64, lo : lo + n] = dot_nt(rows, slope)
                rows = diagonal(
                    (grad_one.astype(F32) * factor[:, :WIN]).astype(BF),
                    (grad_two.astype(F32) * factor[:, WIN:]).astype(BF),
                )
                g_s[w, FEAT + 64 * p : FEAT + 64 * p + 64, lo : lo + n] = dot_nt(rows, low)
            return carry

        lax.fori_loop(0, 4, body, 0)

    backward(2)

    spread = None
    entries = 32 * n_y
    for w in range(4):
        r, c = divmod(w, 2)
        row, lane = iota((entries, WIN), 0), iota((entries, WIN), 1)
        want = jnp.zeros((entries, WIN), jnp.int32)
        for f in range(4):
            want = jnp.where(lane // 32 == f, 32 * far_ref[r, c, f] + lane - 32 * f, want)
        chosen = jnp.where(row == want, 1.0, 0.0).astype(BF)
        term = dot_nt(chosen, g_s[w, :, 3 * WIN : 4 * WIN].astype(BF))
        spread = term if spread is None else spread + term
    pg_out[...] = spread.astype(BF).reshape(n_y, 32, 2 * FEAT)
    pg_copies = [
        remote(pg_out.at[peer], pg_in.at[sy], pg_send, pg_recv, i, sy, {"sy": peer})
        for i, peer in enumerate(peers)
    ]
    pg_arrivals = [
        remote(pg_out.at[peer], pg_in.at[peer], pg_send, pg_recv, i, peer, {"sy": peer})
        for i, peer in enumerate(peers)
    ]
    start_all(pg_copies)

    backward(1)

    def toward(w, code):
        r, c = divmod(w, 2)
        total = None
        for s in range(2):
            here = (adj_ref[r, c, s] == code).astype(F32)
            term = g_s[w, :, (1 + s) * WIN : (2 + s) * WIN] * here
            total = term if total is None else total + term
        return total

    for w in range(4):
        r, c = divmod(w, 2)
        rim_out[2 * r + c] = toward(w, r).astype(BF)
        rim_out[4 + 2 * c + r] = toward(w, 2 + c).astype(BF)

    def rim(src, dst, i, where):
        return remote(
            rim_out.at[pl.ds(src, 2)], rim_in.at[pl.ds(dst, 2)], rim_send, rim_recv, i, i, where
        )

    rims = ((up, rim(0, 2, 0, x_lo)), (down, rim(2, 0, 1, x_hi)), (left, rim(4, 6, 2, y_lo)), (right, rim(6, 4, 3, y_hi)))
    for there, copy in rims:
        pl.when(there)(copy.start)

    backward(0)

    for w in range(4):
        bo_own[w] = dot(owt[mine, :], att[w])

    bo_copy.wait_recv()
    for w in range(4):
        bo_ref[w] = (bo_own[w] + bo_in[w].astype(F32)).astype(BF)

    for there, i, slot in ((up, 1, 0), (down, 0, 2), (left, 3, 4), (right, 2, 6)):

        def none(slot=slot):
            rim_in[slot : slot + 2] = jnp.zeros((2, 2 * FEAT, WIN), BF)

        pl.when(there)(rims[i][1].wait_recv)
        pl.when(jnp.logical_not(there))(none)

    wait_recvs(pg_arrivals)
    coarse = pg_out[sy].astype(F32)
    for peer in peers:
        coarse = coarse + pg_in[peer].astype(F32)
    coarse = (coarse * (1.0 / GRP)).T.astype(BF)

    for w in range(4):
        r, c = divmod(w, 2)
        total = g_s[w, :, :WIN]
        total = total + toward(w ^ 2, r) + toward(w ^ 1, 2 + c)
        total = total + rim_in[2 * r + c].astype(F32) + rim_in[4 + 2 * c + r].astype(F32)
        member = jnp.where(iota((32, WIN), 0) == 8 * w + iota((32, WIN), 1) // GRP, 1.0, 0.0)
        total = total + dot(coarse, member.astype(BF))
        gk_ref[w] = total[:FEAT].astype(BF)
        gv_ref[w] = total[FEAT:].astype(BF)

    for there, copies in halos:
        pl.when(there)(lambda copies=copies: wait_sends(copies))
    wait_sends(pool_copies)
    wait_sends(pg_copies)
    bo_copy.wait_send()
    for there, copy in rims:
        pl.when(there)(copy.wait_send)


def local(n_x, n_y, queries, key_field, value_field, grad_output, out_weight, counts, adjacent, far_list):
    def flat(x):
        return x.reshape(4, -1, WIN)

    vmem = pl.BlockSpec(memory_space=pltpu.VMEM)
    smem = pl.BlockSpec(memory_space=pltpu.SMEM)
    shape = jax.ShapeDtypeStruct((4, FEAT, WIN), BF)
    dma = pltpu.SemaphoreType.DMA
    outs = pl.pallas_call(
        lambda *refs: kernel(n_x, n_y, *refs),
        out_shape=[shape] * 4,
        in_specs=[vmem] * 5 + [smem] * 3,
        out_specs=[vmem] * 4,
        scratch_shapes=[
            pltpu.VMEM((12, BLK, WIN), BF),
            pltpu.VMEM((4, 4, BLK, WIN), BF),
            pltpu.VMEM((4, 512, 256), BF),
            pltpu.VMEM((4, 512, 256), BF),
            pltpu.VMEM((n_y, 32, 2 * FEAT), BF),
            pltpu.VMEM((4, FEAT, WIN), BF),
            pltpu.VMEM((2 * FEAT, FEAT), BF),
            pltpu.VMEM((4, PAIRS, 512, 256), BF),
            pltpu.VMEM((4, PAIRS, 3, 8, 256), F32),
            pltpu.VMEM((4, PAIRS, 3, 80, 256), F32),
            pltpu.VMEM((4, PAIRS, 3, 8, 256), F32),
            pltpu.VMEM((4, PAIRS, 8, 256), F32),
            pltpu.VMEM((4, FEAT, WIN), BF),
            pltpu.VMEM((4, FEAT, WIN), F32),
            pltpu.VMEM((4, 2 * FEAT, 512), F32),
            pltpu.VMEM((n_y, 32, 2 * FEAT), BF),
            pltpu.VMEM((n_y, 32, 2 * FEAT), BF),
            pltpu.VMEM((8, 2 * FEAT, WIN), BF),
            pltpu.VMEM((8, 2 * FEAT, WIN), BF),
            pltpu.VMEM((4, FEAT, WIN), BF),
            pltpu.VMEM((4, FEAT, WIN), BF),
            pltpu.VMEM((4, FEAT, WIN), F32),
            dma((6,)),
            dma((6,)),
            dma((n_y,)),
            dma((n_y,)),
            dma((4,)),
            dma((4,)),
            dma((n_y,)),
            dma((n_y,)),
            dma((1,)),
            dma((1,)),
        ],
        compiler_params=pltpu.CompilerParams(
            collective_id=0, has_side_effects=True, vmem_limit_bytes=48 * 1024 * 1024
        ),
    )(flat(queries), flat(key_field), flat(value_field), flat(grad_output), out_weight, counts, adjacent, far_list)
    block_out, grad_queries, grad_keys, grad_values = outs
    return (
        block_out.reshape(2, 2, FEAT, WIN),
        grad_queries.reshape(queries.shape),
        grad_keys.reshape(queries.shape),
        grad_values.reshape(queries.shape),
    )


def solution(mesh):
    n_x, n_y = mesh.shape["sx"], mesh.shape["sy"]
    grid = P("sx", "sy")
    heads = P("sx", "sy", "hd", None, None)
    return jax.shard_map(
        lambda *args: local(n_x, n_y, *args),
        mesh=mesh,
        in_specs=(heads, heads, heads, grid, P("hd", None), grid, grid, grid),
        out_specs=(P("sx", "sy", "hd", None), heads, heads, heads),
        check_vma=False,
    )
```

```python
import math

import jax
import jax.numpy as jnp
from jax import lax
from jax.experimental import pallas as pl
from jax.experimental.pallas import tpu as pltpu
from jax.sharding import PartitionSpec as P

MESH = pl.DeviceIdType.MESH
BF, F32 = jnp.bfloat16, jnp.float32
WIN = 128
DH = 32
FEAT = 192
AUG = 208
BLK = AUG + FEAT
PAIRS = 3
GRP = 16
VMEM = 63 * 1024 * 1024
MASKED = -1e30
MARK = 1e4
SCALE = 1.0 / math.sqrt(DH)
EXPC = SCALE * math.log2(math.e)
PARTS = ((0, 1), (1, 3), (3, 4))
NT = (((1,), (1,)), ((), ()))


def dot(a, b):
    return jnp.dot(a, b, preferred_element_type=F32)


def dot_nt(a, b):
    return lax.dot_general(a, b, NT, preferred_element_type=F32)


def iota(shape, dim):
    return lax.broadcasted_iota(jnp.int32, shape, dim)


def diagonal(first, second):
    zero = jnp.zeros_like(first)
    return jnp.concatenate(
        [jnp.concatenate([first, zero], 1), jnp.concatenate([zero, second], 1)], 0
    )


def placed(pair, p, tail):
    pieces = [pair]
    if p > 0:
        pieces = [jnp.zeros((64 * p, 256), BF)] + pieces
    if p < PAIRS - 1:
        pieces = pieces + [jnp.zeros((64 * (PAIRS - 1 - p), 256), BF)]
    return jnp.concatenate(pieces + [tail, jnp.zeros((48, 256), BF)], 0)


def neighbours(w):
    r, c = divmod(w, 2)
    return (
        w - 2 if r else 4 + c,
        6 + c if r else w + 2,
        w - 1 if c else 8 + r,
        10 + r if c else w + 1,
    )


def kernel(
    n_x,
    n_y,
    q_in,
    k_in,
    v_in,
    go_in,
    ow_in,
    cnt_in,
    adj_in,
    far_in,
    bo_out_ref,
    gq_out_ref,
    gk_out_ref,
    gv_out_ref,
    cnt_ref,
    adj_ref,
    far_ref,
    q_ref,
    go_ref,
    ow_ref,
    bo_ref,
    gq_ref,
    gk_ref,
    gv_ref,
    kvx,
    keys,
    kt,
    vt,
    pool,
    gm,
    owt,
    e_s,
    m_s,
    a_s,
    f_s,
    c_s,
    att,
    gq_s,
    g_s,
    pg_out,
    pg_in,
    rim_out,
    rim_in,
    bo_out,
    bo_in,
    bo_own,
    halo_send,
    halo_recv,
    pool_send,
    pool_recv,
    rim_send,
    rim_recv,
    pg_send,
    pg_recv,
    bo_send,
    bo_recv,
    in_sem,
    out_sem,
):
    sx, sy, hd = lax.axis_index("sx"), lax.axis_index("sy"), lax.axis_index("hd")
    up, down = sx > 0, sx < n_x - 1
    left, right = sy > 0, sy < n_y - 1
    x_lo, x_hi = {"sx": jnp.maximum(sx - 1, 0)}, {"sx": jnp.minimum(sx + 1, n_x - 1)}
    y_lo, y_hi = {"sy": jnp.maximum(sy - 1, 0)}, {"sy": jnp.minimum(sy + 1, n_y - 1)}
    peers = [lax.rem(sy + off, n_y) for off in range(1, n_y)]

    barrier = pltpu.get_barrier_semaphore()

    def greet(where):
        pl.semaphore_signal(barrier, inc=1, device_id=where, device_id_type=MESH)

    pl.when(up)(lambda: greet(x_lo))
    pl.when(down)(lambda: greet(x_hi))
    greet({"hd": 1 - hd})
    for peer in peers:
        greet({"sy": peer})

    reads = [
        pltpu.make_async_copy(src, dst, in_sem.at[i])
        for i, (src, dst) in enumerate(
            (
                (k_in, kvx.at[pl.ds(0, 4), pl.ds(0, FEAT)]),
                (v_in, kvx.at[pl.ds(0, 4), pl.ds(AUG, FEAT)]),
                (go_in, go_ref),
                (ow_in, ow_ref),
                (q_in, q_ref),
                (adj_in, adj_ref),
                (far_in, far_ref),
                (cnt_in, cnt_ref),
            )
        )
    ]
    for copy in reads:
        copy.start()

    reads[0].wait()
    reads[1].wait()
    reads[7].wait()
    pooled = None
    for w in range(4):
        r, c = divmod(w, 2)
        keep = GRP * cnt_ref[r, c]
        off = (iota((16, WIN), 0) == 0) & (iota((16, WIN), 1) >= keep)
        mask = jnp.where(off, MASKED, 0.0).astype(BF)
        kvx[w, FEAT:AUG] = mask
        block = kvx[w]
        keys[w, 0] = block
        row, lane = iota((32, WIN), 0), iota((32, WIN), 1)
        member = jnp.where(row == 8 * w + lane // GRP, 1.0, 0.0).astype(BF)
        part = dot_nt(member, jnp.concatenate([block[:FEAT], block[AUG:]], 0))
        row, lane = iota((32, 2 * FEAT), 0), iota((32, 2 * FEAT), 1)
        bad = (lane == 0) & (row >= 8 * w + cnt_ref[r, c]) & (row < 8 * w + 8)
        part = jnp.where(bad, MARK, part * (1.0 / GRP))
        pooled = part if pooled is None else pooled + part
    pool[sy] = pooled.astype(BF)

    pl.semaphore_wait(barrier, n_y + up.astype(jnp.int32) + down.astype(jnp.int32))

    def remote(src, dst, sends, recvs, i, j, where):
        return pltpu.make_async_remote_copy(
            src_ref=src,
            dst_ref=dst,
            send_sem=sends.at[i],
            recv_sem=recvs.at[j],
            device_id=where,
            device_id_type=MESH,
        )

    def halo(src, dst, i, where):
        return remote(kvx.at[src], kvx.at[dst], halo_send, halo_recv, i, i, where)

    halos = (
        (up, [halo(pl.ds(0, 2), pl.ds(6, 2), 0, x_lo)]),
        (down, [halo(pl.ds(2, 2), pl.ds(4, 2), 1, x_hi)]),
        (left, [halo(0, 10, 2, y_lo), halo(2, 11, 3, y_lo)]),
        (right, [halo(1, 8, 4, y_hi), halo(3, 9, 5, y_hi)]),
    )
    arrivals = ((up, [1], 4), (down, [0], 6), (left, [4, 5], 8), (right, [2, 3], 10))
    flat = [copy for _, copies in halos for copy in copies]

    def start_all(copies):
        for copy in copies:
            copy.start()

    def wait_sends(copies):
        for copy in copies:
            copy.wait_send()

    def wait_recvs(copies):
        for copy in copies:
            copy.wait_recv()

    pool_copies = [
        remote(pool.at[sy], pool.at[sy], pool_send, pool_recv, i, sy, {"sy": peer})
        for i, peer in enumerate(peers)
    ]
    pool_arrivals = [
        remote(pool.at[peer], pool.at[peer], pool_send, pool_recv, i, peer, {"sy": peer})
        for i, peer in enumerate(peers)
    ]
    for there, copies in halos:
        pl.when(there)(lambda copies=copies: start_all(copies))
    start_all(pool_copies)

    for copy in reads[2:7]:
        copy.wait()
    for w in range(4):
        r, c = divmod(w, 2)
        mixed = dot(ow_ref[...], go_ref[w])
        mixed = jnp.where(iota((FEAT, WIN), 1) < GRP * cnt_ref[r, c], mixed, 0.0)
        gm[w] = mixed.astype(BF)
    owt[...] = ow_ref[...].T

    def turn(w, b, block):
        pad = jnp.zeros((48, WIN), BF)
        kt[w, pl.ds(WIN * b, WIN), :] = jnp.concatenate([block[:AUG], pad], 0).T
        vt[w, pl.ds(WIN * b, WIN), :] = jnp.concatenate(
            [block[AUG:], jnp.zeros((64, WIN), BF)], 0
        ).T

    for w in range(4):
        turn(w, 0, keys[w, 0])

    def rows_of(w, part, base, p):
        first, last = PARTS[part]
        return jnp.concatenate(
            [keys[w, b, base + 64 * p : base + 64 * p + 64, :] for b in range(first, last)], 1
        )

    def forward(part):
        first, last = PARTS[part]
        lo, n = WIN * first, WIN * (last - first)
        one_row = jnp.where(iota((16, 256), 0) == 0, 1.0, 0.0).astype(BF)
        ones = jnp.ones((16, n), BF)

        def body(w, carry):
            scores, tops, lows, sums = [], [], [], []
            for p in range(PAIRS):
                pair = diagonal(
                    q_ref[w, 64 * p : 64 * p + 32, :], q_ref[w, 64 * p + 32 : 64 * p + 64, :]
                )
                scores.append(dot(kt[w, lo : lo + n, :], placed(pair, p, one_row)))
            rows = [jnp.concatenate([rows_of(w, part, AUG, p), ones], 0) for p in range(PAIRS)]
            for p in range(PAIRS):
                tops.append(jnp.max(scores[p], axis=0, keepdims=True))
                lows.append(jnp.exp2((scores[p] - tops[p]) * EXPC).astype(BF))
            for p in range(PAIRS):
                sums.append(dot(rows[p], lows[p]))
            for p in range(PAIRS):
                e_s[w, p, lo : lo + n, :] = lows[p]
                a_s[w, p, part] = sums[p]
                m_s[w, p, part] = jnp.broadcast_to(tops[p], (8, 256))
            return carry

        lax.fori_loop(0, 4, body, 0, unroll=4)

    forward(0)

    for there, index, slot in arrivals:

        def arrive(index=index):
            wait_recvs([flat[i] for i in index])

        def outside(slot=slot):
            off = iota((2, BLK, WIN), 1) == FEAT
            kvx[slot : slot + 2] = jnp.where(off, MASKED, 0.0).astype(BF)

        pl.when(there)(arrive)
        pl.when(jnp.logical_not(there))(outside)

    for w in range(4):
        r, c = divmod(w, 2)
        n0, n1, n2, n3 = neighbours(w)
        for s in range(2):
            code = adj_ref[r, c, s]
            slot = jnp.where(
                code < 2, jnp.where(code == 0, n0, n1), jnp.where(code == 2, n2, n3)
            )
            block = kvx[slot]
            keys[w, 1 + s] = block
            turn(w, 1 + s, block)

    forward(1)

    wait_recvs(pool_arrivals)
    for w in range(4):
        r, c = divmod(w, 2)
        listed = jnp.concatenate([pool[far_ref[r, c, f]] for f in range(4)], 0).T
        bad = (iota((16, WIN), 0) == 0) & (listed[:16].astype(F32) > 0.5 * MARK)
        mask = jnp.where(bad, MASKED, 0.0).astype(BF)
        block = jnp.concatenate([listed[:FEAT], mask, listed[FEAT:]], 0)
        keys[w, 3] = block
        turn(w, 3, block)

    forward(2)

    def combine(w, carry):
        keep = GRP * cnt_ref[w // 2, w % 2]
        for p in range(PAIRS):
            tops = [m_s[w, p, i, 0:1, :] for i in range(3)]
            top = jnp.maximum(jnp.maximum(tops[0], tops[1]), tops[2])
            shares = [jnp.exp2((t - top) * EXPC) for t in tops]
            total = sum(share * a_s[w, p, i] for i, share in enumerate(shares))
            inverse = 1.0 / total[64:65]
            first = total[:32, :WIN] * inverse[:, :WIN]
            second = total[32:64, WIN:] * inverse[:, WIN:]
            both = jnp.concatenate([first, second], 0)
            product = both * gm[w, 64 * p : 64 * p + 64, :].astype(F32)
            centre = jnp.concatenate(
                [
                    jnp.sum(product[:32], axis=0, keepdims=True),
                    jnp.sum(product[32:], axis=0, keepdims=True),
                ],
                1,
            )
            c_s[w, p] = jnp.broadcast_to(centre, (8, 256))
            for i, share in enumerate(shares):
                f_s[w, p, i] = jnp.broadcast_to(share * inverse, (8, 256))
            both = jnp.where(iota((64, WIN), 1) < keep, both, 0.0)
            att[w, 64 * p : 64 * p + 64, :] = both.astype(BF)
        return carry

    lax.fori_loop(0, 4, combine, 0)

    mine = pl.ds(pl.multiple_of(hd * FEAT, FEAT), FEAT)
    theirs = pl.ds(pl.multiple_of((1 - hd) * FEAT, FEAT), FEAT)
    for w in range(4):
        bo_out[w] = dot(owt[theirs, :], att[w]).astype(BF)
    bo_copy = remote(bo_out, bo_in, bo_send, bo_recv, 0, 0, {"hd": 1 - hd})
    bo_copy.start()

    def backward(part):
        first, last = PARTS[part]
        lo, n = WIN * first, WIN * (last - first)
        no_row = jnp.zeros((16, 256), BF)

        def body(w, carry):
            factors = [f_s[w, p, part, 0:1, :] for p in range(PAIRS)]
            lows = [e_s[w, p, lo : lo + n, :] for p in range(PAIRS)]
            olds = [gq_s[w, 64 * p : 64 * p + 64, :] for p in range(PAIRS)]
            slopes, backs, key_terms, value_terms = [], [], [], []
            heads = [
                (q_ref[w, 32 * h : 32 * h + 32, :], gm[w, 32 * h : 32 * h + 32, :])
                for h in range(2 * PAIRS)
            ]
            keyrows = [rows_of(w, part, 0, p) for p in range(PAIRS)]
            for p in range(PAIRS):
                pair = diagonal(heads[2 * p][1], heads[2 * p + 1][1])
                prob = dot(vt[w, lo : lo + n, :], placed(pair, p, no_row))
                slopes.append((lows[p].astype(F32) * (prob - c_s[w, p, 0:1, :])).astype(BF))
            for p in range(PAIRS):
                scaled = factors[p] * SCALE
                (q_one, grad_one), (q_two, grad_two) = heads[2 * p], heads[2 * p + 1]
                back = dot(keyrows[p], slopes[p]) * scaled
                backs.append(jnp.concatenate([back[:32, :WIN], back[32:, WIN:]], 0))
                rows = diagonal(
                    (q_one.astype(F32) * scaled[:, :WIN]).astype(BF),
                    (q_two.astype(F32) * scaled[:, WIN:]).astype(BF),
                )
                key_terms.append(dot_nt(rows, slopes[p]))
                rows = diagonal(
                    (grad_one.astype(F32) * factors[p][:, :WIN]).astype(BF),
                    (grad_two.astype(F32) * factors[p][:, WIN:]).astype(BF),
                )
                value_terms.append(dot_nt(rows, lows[p]))
            for p in range(PAIRS):
                at = slice(64 * p, 64 * p + 64)
                back = backs[p] if part == 2 else backs[p] + olds[p]
                if part == 0:
                    gq_ref[w, at, :] = back.astype(BF)
                else:
                    gq_s[w, at, :] = back
                g_s[w, at, lo : lo + n] = key_terms[p]
                g_s[w, FEAT + 64 * p : FEAT + 64 * p + 64, lo : lo + n] = value_terms[p]
            return carry

        lax.fori_loop(0, 4, body, 0, unroll=4)

    backward(2)

    spread = None
    entries = 32 * n_y
    for w in range(4):
        r, c = divmod(w, 2)
        row, lane = iota((entries, WIN), 0), iota((entries, WIN), 1)
        want = jnp.zeros((entries, WIN), jnp.int32)
        for f in range(4):
            want = jnp.where(lane // 32 == f, 32 * far_ref[r, c, f] + lane - 32 * f, want)
        chosen = jnp.where(row == want, 1.0, 0.0).astype(BF)
        term = dot_nt(chosen, g_s[w, :, 3 * WIN : 4 * WIN].astype(BF))
        spread = term if spread is None else spread + term
    pg_out[...] = spread.astype(BF).reshape(n_y, 32, 2 * FEAT)
    pg_copies = [
        remote(pg_out.at[peer], pg_in.at[sy], pg_send, pg_recv, i, sy, {"sy": peer})
        for i, peer in enumerate(peers)
    ]
    pg_arrivals = [
        remote(pg_out.at[peer], pg_in.at[peer], pg_send, pg_recv, i, peer, {"sy": peer})
        for i, peer in enumerate(peers)
    ]
    start_all(pg_copies)

    backward(1)

    def toward(w, code):
        r, c = divmod(w, 2)
        total = None
        for s in range(2):
            here = (adj_ref[r, c, s] == code).astype(F32)
            term = g_s[w, :, (1 + s) * WIN : (2 + s) * WIN] * here
            total = term if total is None else total + term
        return total

    for w in range(4):
        r, c = divmod(w, 2)
        rim_out[2 * r + c] = toward(w, r).astype(BF)
        rim_out[4 + 2 * c + r] = toward(w, 2 + c).astype(BF)

    def rim(src, dst, i, where):
        return remote(
            rim_out.at[pl.ds(src, 2)], rim_in.at[pl.ds(dst, 2)], rim_send, rim_recv, i, i, where
        )

    rims = ((up, rim(0, 2, 0, x_lo)), (down, rim(2, 0, 1, x_hi)), (left, rim(4, 6, 2, y_lo)), (right, rim(6, 4, 3, y_hi)))
    for there, copy in rims:
        pl.when(there)(copy.start)

    backward(0)

    for w in range(4):
        bo_own[w] = dot(owt[mine, :], att[w])

    writes = [
        pltpu.make_async_copy(src, dst, out_sem.at[i])
        for i, (src, dst) in enumerate(
            ((gq_ref, gq_out_ref), (bo_ref, bo_out_ref), (gk_ref, gk_out_ref), (gv_ref, gv_out_ref))
        )
    ]
    writes[0].start()

    bo_copy.wait_recv()
    for w in range(4):
        bo_ref[w] = (bo_own[w] + bo_in[w].astype(F32)).astype(BF)
    writes[1].start()

    for there, i, slot in ((up, 1, 0), (down, 0, 2), (left, 3, 4), (right, 2, 6)):

        def none(slot=slot):
            rim_in[slot : slot + 2] = jnp.zeros((2, 2 * FEAT, WIN), BF)

        pl.when(there)(rims[i][1].wait_recv)
        pl.when(jnp.logical_not(there))(none)

    wait_recvs(pg_arrivals)
    coarse = pg_out[sy].astype(F32)
    for peer in peers:
        coarse = coarse + pg_in[peer].astype(F32)
    coarse = (coarse * (1.0 / GRP)).T.astype(BF)

    for w in range(4):
        r, c = divmod(w, 2)
        total = g_s[w, :, :WIN]
        total = total + toward(w ^ 2, r) + toward(w ^ 1, 2 + c)
        total = total + rim_in[2 * r + c].astype(F32) + rim_in[4 + 2 * c + r].astype(F32)
        member = jnp.where(iota((32, WIN), 0) == 8 * w + iota((32, WIN), 1) // GRP, 1.0, 0.0)
        total = total + dot(coarse, member.astype(BF))
        gk_ref[w] = total[:FEAT].astype(BF)
        gv_ref[w] = total[FEAT:].astype(BF)
    writes[2].start()
    writes[3].start()

    for there, copies in halos:
        pl.when(there)(lambda copies=copies: wait_sends(copies))
    wait_sends(pool_copies)
    wait_sends(pg_copies)
    bo_copy.wait_send()
    for there, copy in rims:
        pl.when(there)(copy.wait_send)
    for copy in writes:
        copy.wait()


def hand_over(*refs):
    copies = [
        pltpu.make_async_copy(refs[i], refs[4 + i], refs[8].at[i]) for i in range(4)
    ]
    for copy in copies:
        copy.start()
    for copy in copies:
        copy.wait()


def local(n_x, n_y, queries, key_field, value_field, grad_output, out_weight, counts, adjacent, far_list):
    def flat(x):
        return x.reshape(4, -1, WIN)

    vmem = pl.BlockSpec(memory_space=pltpu.VMEM)
    hbm = pl.BlockSpec(memory_space=pl.ANY)
    shape = jax.ShapeDtypeStruct((4, FEAT, WIN), BF)
    dma = pltpu.SemaphoreType.DMA
    outs = pl.pallas_call(
        lambda *refs: kernel(n_x, n_y, *refs),
        out_shape=[shape] * 4,
        in_specs=[hbm] * 8,
        out_specs=[hbm] * 4,
        scratch_shapes=[
            pltpu.SMEM(counts.shape, jnp.int32),
            pltpu.SMEM(adjacent.shape, jnp.int32),
            pltpu.SMEM(far_list.shape, jnp.int32),
            pltpu.VMEM((4, FEAT, WIN), BF),
            pltpu.VMEM((4, 2 * FEAT, WIN), BF),
            pltpu.VMEM((FEAT, 2 * FEAT), BF),
            pltpu.VMEM((4, FEAT, WIN), BF),
            pltpu.VMEM((4, FEAT, WIN), BF),
            pltpu.VMEM((4, FEAT, WIN), BF),
            pltpu.VMEM((4, FEAT, WIN), BF),
            pltpu.VMEM((12, BLK, WIN), BF),
            pltpu.VMEM((4, 4, BLK, WIN), BF),
            pltpu.VMEM((4, 512, 256), BF),
            pltpu.VMEM((4, 512, 256), BF),
            pltpu.VMEM((n_y, 32, 2 * FEAT), BF),
            pltpu.VMEM((4, FEAT, WIN), BF),
            pltpu.VMEM((2 * FEAT, FEAT), BF),
            pltpu.VMEM((4, PAIRS, 512, 256), BF),
            pltpu.VMEM((4, PAIRS, 3, 8, 256), F32),
            pltpu.VMEM((4, PAIRS, 3, 80, 256), F32),
            pltpu.VMEM((4, PAIRS, 3, 8, 256), F32),
            pltpu.VMEM((4, PAIRS, 8, 256), F32),
            pltpu.VMEM((4, FEAT, WIN), BF),
            pltpu.VMEM((4, FEAT, WIN), F32),
            pltpu.VMEM((4, 2 * FEAT, 512), F32),
            pltpu.VMEM((n_y, 32, 2 * FEAT), BF),
            pltpu.VMEM((n_y, 32, 2 * FEAT), BF),
            pltpu.VMEM((8, 2 * FEAT, WIN), BF),
            pltpu.VMEM((8, 2 * FEAT, WIN), BF),
            pltpu.VMEM((4, FEAT, WIN), BF),
            pltpu.VMEM((4, FEAT, WIN), BF),
            pltpu.VMEM((4, FEAT, WIN), F32),
            dma((6,)),
            dma((6,)),
            dma((n_y,)),
            dma((n_y,)),
            dma((4,)),
            dma((4,)),
            dma((n_y,)),
            dma((n_y,)),
            dma((1,)),
            dma((1,)),
            dma((8,)),
            dma((4,)),
        ],
        compiler_params=pltpu.CompilerParams(
            collective_id=0, has_side_effects=True, vmem_limit_bytes=VMEM
        ),
    )(flat(queries), flat(key_field), flat(value_field), flat(grad_output), out_weight, counts, adjacent, far_list)
    block_out, grad_queries, grad_keys, grad_values = pl.pallas_call(
        hand_over,
        out_shape=[shape] * 4,
        in_specs=[vmem] * 4,
        out_specs=[hbm] * 4,
        scratch_shapes=[dma((4,))],
        compiler_params=pltpu.CompilerParams(vmem_limit_bytes=VMEM),
    )(*outs)
    return (
        block_out.reshape(2, 2, FEAT, WIN),
        grad_queries.reshape(queries.shape),
        grad_keys.reshape(queries.shape),
        grad_values.reshape(queries.shape),
    )


def solution(mesh):
    n_x, n_y = mesh.shape["sx"], mesh.shape["sy"]
    grid = P("sx", "sy")
    heads = P("sx", "sy", "hd", None, None)
    return jax.shard_map(
        lambda *args: local(n_x, n_y, *args),
        mesh=mesh,
        in_specs=(heads, heads, heads, grid, P("hd", None), grid, grid, grid),
        out_specs=(P("sx", "sy", "hd", None), heads, heads, heads),
        check_vma=False,
    )
```

```python
import math

import jax
import jax.numpy as jnp
from jax import lax
from jax.experimental import pallas as pl
from jax.experimental.pallas import tpu as pltpu
from jax.sharding import PartitionSpec as P

MESH = pl.DeviceIdType.MESH
BF, F32 = jnp.bfloat16, jnp.float32
WIN = 128
DH = 32
FEAT = 192
AUG = 208
PAIRS = 3
GRP = 16
VMEM = 63 * 1024 * 1024
MASKED = -1e30
MARK = 1e4
SCALE = 1.0 / math.sqrt(DH)
EXPC = SCALE * math.log2(math.e)
PARTS = ((0, 1), (1, 3), (3, 4))
NT = (((1,), (1,)), ((), ()))


def dot(a, b):
    return jnp.dot(a, b, preferred_element_type=F32)


def dot_nt(a, b):
    return lax.dot_general(a, b, NT, preferred_element_type=F32)


def iota(shape, dim):
    return lax.broadcasted_iota(jnp.int32, shape, dim)


def diagonal(first, second):
    zero = jnp.zeros_like(first)
    return jnp.concatenate(
        [jnp.concatenate([first, zero], 1), jnp.concatenate([zero, second], 1)], 0
    )


def placed(pair, p, tail):
    pieces = [pair]
    if p > 0:
        pieces = [jnp.zeros((64 * p, 256), BF)] + pieces
    if p < PAIRS - 1:
        pieces = pieces + [jnp.zeros((64 * (PAIRS - 1 - p), 256), BF)]
    return jnp.concatenate(pieces + [tail, jnp.zeros((48, 256), BF)], 0)


def neighbours(w):
    r, c = divmod(w, 2)
    return (
        w - 2 if r else 4 + c,
        6 + c if r else w + 2,
        w - 1 if c else 8 + r,
        10 + r if c else w + 1,
    )


def pack(x):
    tail = jnp.concatenate([x[:, :16, WIN:], x[:, 16:, WIN:]], 2)
    return jnp.concatenate([x[:, :, :WIN], tail], 1)


def unpack(x):
    tail = jnp.concatenate([x[32:, :64], x[32:, 64:]], 0)
    return jnp.concatenate([x[:32], tail], 1)


def kernel(
    n_x,
    n_y,
    q_in,
    k_in,
    v_in,
    go_in,
    ow_in,
    cnt_in,
    adj_in,
    far_in,
    bo_out_ref,
    gq_out_ref,
    gk_out_ref,
    gv_out_ref,
    cnt_ref,
    adj_ref,
    far_ref,
    q_ref,
    go_ref,
    ow_ref,
    bo_ref,
    gq_ref,
    gk_ref,
    gv_ref,
    kx,
    vx,
    kk,
    vv,
    kt,
    vt,
    pool_k,
    pool_v,
    gm,
    owt,
    e_s,
    m_s,
    a_s,
    f_s,
    c_s,
    att,
    gq_s,
    g_s,
    pg_out,
    pg_half,
    pg_sum,
    pg_in,
    rim_out,
    rim_in,
    bo_out,
    bo_in,
    bo_own,
    halo_send,
    halo_recv,
    pool_send,
    pool_recv,
    rim_send,
    rim_recv,
    pg_send,
    pg_recv,
    half_send,
    half_recv,
    bo_send,
    bo_recv,
    in_sem,
    out_sem,
):
    sx, sy, hd = lax.axis_index("sx"), lax.axis_index("sy"), lax.axis_index("hd")
    up, down = sx > 0, sx < n_x - 1
    left, right = sy > 0, sy < n_y - 1
    x_lo, x_hi = {"sx": jnp.maximum(sx - 1, 0)}, {"sx": jnp.minimum(sx + 1, n_x - 1)}
    y_lo, y_hi = {"sy": jnp.maximum(sy - 1, 0)}, {"sy": jnp.minimum(sy + 1, n_y - 1)}
    n_z = n_y // 2
    z, core = sy // 2, lax.rem(sy, 2)
    sibling = {"sy": sy + 1 - 2 * core}
    outer = {"sy": lax.rem(sy + 2 * core - 1 + n_y, n_y)}
    partner = {"hd": 1 - hd}

    def chip_at(step):
        return lax.rem(z + step + n_z, n_z)

    barrier = pltpu.get_barrier_semaphore()

    def greet(where):
        pl.semaphore_signal(barrier, inc=1, device_id=where, device_id_type=MESH)

    steps = sorted(range(1, n_z), key=lambda step: -min(step, n_z - step))
    others = [chip_at(step) for step in steps]
    for chip in others:
        greet({"sy": 2 * chip + core})
    pl.when(up)(lambda: greet(x_lo))
    pl.when(down)(lambda: greet(x_hi))
    for where in (partner, outer, sibling):
        greet(where)

    reads = [
        pltpu.make_async_copy(src, dst, in_sem.at[i])
        for i, (src, dst) in enumerate(
            (
                (k_in, kx.at[pl.ds(0, 4), pl.ds(0, FEAT)]),
                (v_in, vx.at[pl.ds(0, 4)]),
                (cnt_in, cnt_ref),
                (go_in, go_ref),
                (ow_in, ow_ref),
                (q_in, q_ref),
                (adj_in, adj_ref),
                (far_in, far_ref),
            )
        )
    ]
    for copy in reads:
        copy.start()

    for copy in reads[:3]:
        copy.wait()
    pooled_k = pooled_v = None
    for w in range(4):
        r, c = divmod(w, 2)
        keep = GRP * cnt_ref[r, c]
        off = (iota((16, WIN), 0) == 0) & (iota((16, WIN), 1) >= keep)
        kx[w, FEAT:AUG] = jnp.where(off, MASKED, 0.0).astype(BF)
        row, lane = iota((32, WIN), 0), iota((32, WIN), 1)
        member = jnp.where(row == 8 * w + lane // GRP, 1.0, 0.0).astype(BF)
        row, lane = iota((32, FEAT), 0), iota((32, FEAT), 1)
        bad = (lane == 0) & (row >= 8 * w + cnt_ref[r, c]) & (row < 8 * w + 8)
        part = dot_nt(member, kx[w, 0:FEAT]) * (1.0 / GRP)
        part = jnp.where(bad, MARK, part)
        pooled_k = part if pooled_k is None else pooled_k + part
        part = dot_nt(member, vx[w]) * (1.0 / GRP)
        pooled_v = part if pooled_v is None else pooled_v + part
    pool_k[z, core] = pack(pooled_k[None])[0].astype(BF)
    pool_v[z, core] = pack(pooled_v[None])[0].astype(BF)

    pl.semaphore_wait(barrier, n_z + 2 + up.astype(jnp.int32) + down.astype(jnp.int32))

    def remote(src, dst, sends, recvs, i, j, where):
        return pltpu.make_async_remote_copy(
            src_ref=src,
            dst_ref=dst,
            send_sem=sends.at[i],
            recv_sem=recvs.at[j],
            device_id=where,
            device_id_type=MESH,
        )

    def start_all(copies):
        for copy in copies:
            copy.start()

    def wait_sends(copies):
        for copy in copies:
            copy.wait_send()

    def wait_recvs(copies):
        for copy in copies:
            copy.wait_recv()

    def halo_copies(ref, base):
        def halo(src, dst, i, where):
            return remote(ref.at[src], ref.at[dst], halo_send, halo_recv, base + i, base + i, where)

        return (
            (up, [halo(pl.ds(0, 2), pl.ds(6, 2), 0, x_lo)]),
            (down, [halo(pl.ds(2, 2), pl.ds(4, 2), 1, x_hi)]),
            (left, [halo(0, 10, 2, y_lo), halo(2, 11, 3, y_lo)]),
            (right, [halo(1, 8, 4, y_hi), halo(3, 9, 5, y_hi)]),
        )

    halos = [halo_copies(kx, 0), halo_copies(vx, 6)]

    def start_halos(which):
        for there, copies in halos[which]:
            pl.when(there)(lambda copies=copies: start_all(copies))

    def halos_arrive(which, ref, fill):
        flat = [copy for _, copies in halos[which] for copy in copies]
        for there, index, slot in ((up, [1], 4), (down, [0], 6), (left, [4, 5], 8), (right, [2, 3], 10)):

            def arrive(index=index):
                wait_recvs([flat[i] for i in index])

            def outside(slot=slot):
                ref[slot : slot + 2] = fill

            pl.when(there)(arrive)
            pl.when(jnp.logical_not(there))(outside)

    pools = (pool_k, pool_v)
    started = ([], [])

    def pooled_copy(which, chip, part, i, where):
        block = pools[which].at[chip, part]
        base = n_y * which
        return remote(block, block, pool_send, pool_recv, base + i, base + 2 * chip + part, where)

    def send_pooled(which, chip, where):
        copy = pooled_copy(which, chip, core, len(started[which]), where)
        copy.start()
        started[which].append(copy)

    def pass_on(which):
        for chip in reversed(others):
            pooled_copy(which, chip, core, 0, sibling).wait_recv()
            send_pooled(which, chip, sibling)

    def handed(which):
        for chip in [z] + others:
            pooled_copy(which, chip, 1 - core, 0, sibling).wait_recv()

    for which in range(2):
        for chip in others:
            send_pooled(which, z, {"sy": 2 * chip + core})
        start_halos(which)
    for which in range(2):
        send_pooled(which, z, sibling)

    def turn_keys(w, b, block):
        pad = jnp.zeros((48, WIN), BF)
        kt[w, pl.ds(WIN * b, WIN), :] = jnp.concatenate([block, pad], 0).T

    def turn_values(w, b, block):
        pad = jnp.zeros((64, WIN), BF)
        vt[w, pl.ds(WIN * b, WIN), :] = jnp.concatenate([block, pad], 0).T

    for copy in reads[3:]:
        copy.wait()
    for w in range(4):
        kk[w, 0] = kx[w]
        vv[w, 0] = vx[w]
        turn_keys(w, 0, kx[w])
        turn_values(w, 0, vx[w])

    def rows_of(ref, w, part, p):
        first, last = PARTS[part]
        return jnp.concatenate(
            [ref[w, b, 64 * p : 64 * p + 64, :] for b in range(first, last)], 1
        )

    def span(part):
        first, last = PARTS[part]
        return slice(WIN * first, WIN * last)

    every = [(w, p) for w in range(4) for p in range(PAIRS)]

    def head(ref, w, h):
        return ref[w, 32 * h : 32 * h + 32, :]

    def score(part):
        one_row = jnp.where(iota((16, 256), 0) == 0, 1.0, 0.0).astype(BF)
        at = span(part)
        for w in range(4):
            pairs = [diagonal(head(q_ref, w, 2 * p), head(q_ref, w, 2 * p + 1)) for p in range(PAIRS)]
            scores = [dot(kt[w, at, :], placed(pairs[p], p, one_row)) for p in range(PAIRS)]
            tops = [jnp.max(x, axis=0, keepdims=True) for x in scores]
            lows = [jnp.exp2((x - top) * EXPC).astype(BF) for x, top in zip(scores, tops)]
            for p in range(PAIRS):
                e_s[w, p, at, :] = lows[p]
                m_s[w, p, part] = jnp.broadcast_to(tops[p], (8, 256))

    def weigh(part):
        ones = jnp.ones((16, WIN * (PARTS[part][1] - PARTS[part][0])), BF)
        for w, p in every:
            rows = jnp.concatenate([rows_of(vv, w, part, p), ones], 0)
            a_s[w, p, part] = dot(rows, e_s[w, p, span(part), :])

    score(0)
    weigh(0)

    for w in range(4):
        r, c = divmod(w, 2)
        mixed = dot(ow_ref[...], go_ref[w])
        mixed = jnp.where(iota((FEAT, WIN), 1) < GRP * cnt_ref[r, c], mixed, 0.0)
        gm[w] = mixed.astype(BF)
    owt[...] = ow_ref[...].T

    def beside_slot(w, s):
        r, c = divmod(w, 2)
        n0, n1, n2, n3 = neighbours(w)
        code = adj_ref[r, c, s]
        return jnp.where(code < 2, jnp.where(code == 0, n0, n1), jnp.where(code == 2, n2, n3))

    def listed(which, w):
        r, c = divmod(w, 2)
        far = [far_ref[r, c, f] for f in range(4)]
        return jnp.concatenate([unpack(pools[which][e // 2, e % 2]) for e in far], 0).T

    pass_on(0)
    halos_arrive(0, kx, jnp.where(iota((2, AUG, WIN), 1) == FEAT, MASKED, 0.0).astype(BF))
    for w in range(4):
        for s in range(2):
            block = kx[beside_slot(w, s)]
            kk[w, 1 + s] = block
            turn_keys(w, 1 + s, block)
    score(1)

    handed(0)
    for w in range(4):
        rows = listed(0, w)
        bad = (iota((16, WIN), 0) == 0) & (rows[:16].astype(F32) > 0.5 * MARK)
        block = jnp.concatenate([rows, jnp.where(bad, MASKED, 0.0).astype(BF)], 0)
        kk[w, 3] = block
        turn_keys(w, 3, block)
    pass_on(1)
    score(2)

    halos_arrive(1, vx, jnp.zeros((2, FEAT, WIN), BF))
    for w in range(4):
        for s in range(2):
            block = vx[beside_slot(w, s)]
            vv[w, 1 + s] = block
            turn_values(w, 1 + s, block)
    weigh(1)
    handed(1)
    for w in range(4):
        block = listed(1, w)
        vv[w, 3] = block
        turn_values(w, 3, block)
    weigh(2)

    for w, p in every:
        keep = GRP * cnt_ref[w // 2, w % 2]
        tops = [m_s[w, p, i, 0:1, :] for i in range(3)]
        top = jnp.maximum(jnp.maximum(tops[0], tops[1]), tops[2])
        shares = [jnp.exp2((t - top) * EXPC) for t in tops]
        total = sum(share * a_s[w, p, i] for i, share in enumerate(shares))
        inverse = 1.0 / total[64:65]
        first = total[:32, :WIN] * inverse[:, :WIN]
        second = total[32:64, WIN:] * inverse[:, WIN:]
        both = jnp.concatenate([first, second], 0)
        product = both * gm[w, 64 * p : 64 * p + 64, :].astype(F32)
        centre = jnp.concatenate(
            [
                jnp.sum(product[:32], axis=0, keepdims=True),
                jnp.sum(product[32:], axis=0, keepdims=True),
            ],
            1,
        )
        c_s[w, p] = jnp.broadcast_to(centre, (8, 256))
        for i, share in enumerate(shares):
            f_s[w, p, i] = jnp.broadcast_to(share * inverse, (8, 256))
        both = jnp.where(iota((64, WIN), 1) < keep, both, 0.0)
        att[w, 64 * p : 64 * p + 64, :] = both.astype(BF)

    def scaled_heads(ref, w, p, factor):
        return diagonal(
            (head(ref, w, 2 * p).astype(F32) * factor[:, :WIN]).astype(BF),
            (head(ref, w, 2 * p + 1).astype(F32) * factor[:, WIN:]).astype(BF),
        )

    def value_terms(part):
        at = span(part)
        for w, p in every:
            rows = scaled_heads(gm, w, p, f_s[w, p, part, 0:1, :])
            g_s[w, FEAT + 64 * p : FEAT + 64 * p + 64, at] = dot_nt(rows, e_s[w, p, at, :])

    def key_terms(part):
        no_row = jnp.zeros((16, 256), BF)
        at = span(part)
        for w in range(4):
            slopes, backs, terms = [], [], []
            lows = [e_s[w, p, at, :] for p in range(PAIRS)]
            olds = [gq_s[w, 64 * p : 64 * p + 64, :] for p in range(PAIRS)]
            for p in range(PAIRS):
                pair = diagonal(head(gm, w, 2 * p), head(gm, w, 2 * p + 1))
                prob = dot(vt[w, at, :], placed(pair, p, no_row))
                slopes.append((lows[p].astype(F32) * (prob - c_s[w, p, 0:1, :])).astype(BF))
            for p in range(PAIRS):
                scaled = f_s[w, p, part, 0:1, :] * SCALE
                back = dot(rows_of(kk, w, part, p), slopes[p]) * scaled
                backs.append(jnp.concatenate([back[:32, :WIN], back[32:, WIN:]], 0))
                terms.append(dot_nt(scaled_heads(q_ref, w, p, scaled), slopes[p]))
            for p in range(PAIRS):
                rows = slice(64 * p, 64 * p + 64)
                back = backs[p] if part == 2 else backs[p] + olds[p]
                if part == 0:
                    gq_ref[w, rows, :] = back.astype(BF)
                else:
                    gq_s[w, rows, :] = back
                g_s[w, rows, at] = terms[p]

    entries = 32 * n_y
    chosen = []
    for w in range(4):
        row, lane = iota((entries, WIN), 0), iota((entries, WIN), 1)
        want = jnp.zeros((entries, WIN), jnp.int32)
        for f in range(4):
            code = far_ref[w // 2, w % 2, f]
            want = jnp.where(lane // 32 == f, 32 * code + lane - 32 * f, want)
        chosen.append(jnp.where(row == want, 1.0, 0.0).astype(BF))

    def half_copy(which):
        return remote(
            pg_out.at[which, :, 1 - core], pg_half.at[which], half_send, half_recv, which, which, sibling
        )

    def send_half(which):
        spread = None
        for w in range(4):
            term = dot_nt(chosen[w], g_s[w, FEAT * which : FEAT * which + FEAT, 3 * WIN :].astype(BF))
            spread = term if spread is None else spread + term
        spread = pack(spread.reshape(n_y, 32, FEAT)).astype(BF)
        pg_out[which] = spread.reshape(n_z, 2, 48, WIN)
        half_copy(which).start()

    def pg_copy(which, i, src, dst, where):
        i, j = n_z * which + i, n_z * which + dst
        return remote(pg_sum.at[which, src], pg_in.at[which, dst], pg_send, pg_recv, i, j, where)

    def pg_sends(which):
        return [
            pg_copy(which, i, chip_at(step), z, {"sy": 2 * chip_at(step) + core})
            for i, step in enumerate(steps)
        ]

    def send_owners(which):
        half_copy(which).wait_recv()
        both = pg_out[which, :, core].astype(F32) + pg_half[which].astype(F32)
        pg_sum[which] = both.astype(BF)
        start_all(pg_sends(which))

    def toward(w, code, which):
        r, c = divmod(w, 2)
        total = None
        for s in range(2):
            here = (adj_ref[r, c, s] == code).astype(F32)
            term = g_s[w, FEAT * which : FEAT * which + FEAT, (1 + s) * WIN : (2 + s) * WIN] * here
            total = term if total is None else total + term
        return total

    def rims(which):
        def rim(src, dst, i, where):
            rows = pl.ds(FEAT * which, FEAT)
            i = 4 * which + i
            return remote(
                rim_out.at[pl.ds(src, 2), rows],
                rim_in.at[pl.ds(dst, 2), rows],
                rim_send,
                rim_recv,
                i,
                i,
                where,
            )

        return (
            (up, rim(0, 2, 0, x_lo)),
            (down, rim(2, 0, 1, x_hi)),
            (left, rim(4, 6, 2, y_lo)),
            (right, rim(6, 4, 3, y_hi)),
        )

    def send_rims(which):
        at = slice(FEAT * which, FEAT * which + FEAT)
        for w in range(4):
            r, c = divmod(w, 2)
            rim_out[2 * r + c, at] = toward(w, r, which).astype(BF)
            rim_out[4 + 2 * c + r, at] = toward(w, 2 + c, which).astype(BF)
        for there, copy in rims(which):
            pl.when(there)(copy.start)

    value_terms(2)
    send_half(1)

    mine = pl.ds(pl.multiple_of(hd * FEAT, FEAT), FEAT)
    theirs = pl.ds(pl.multiple_of((1 - hd) * FEAT, FEAT), FEAT)
    for w in range(4):
        bo_out[w] = dot(owt[theirs, :], att[w]).astype(BF)
    share = remote(bo_out, bo_in, bo_send, bo_recv, 0, 0, partner)
    share.start()

    value_terms(1)
    send_rims(1)
    send_owners(1)
    key_terms(2)
    send_half(0)
    value_terms(0)
    send_owners(0)
    key_terms(1)
    send_rims(0)
    key_terms(0)

    writes = [
        pltpu.make_async_copy(src, dst, out_sem.at[i])
        for i, (src, dst) in enumerate(
            ((gq_ref, gq_out_ref), (bo_ref, bo_out_ref), (gk_ref, gk_out_ref), (gv_ref, gv_out_ref))
        )
    ]
    writes[0].start()

    for w in range(4):
        bo_own[w] = dot(owt[mine, :], att[w])

    share.wait_recv()
    for w in range(4):
        bo_ref[w] = (bo_own[w] + bo_in[w].astype(F32)).astype(BF)
    writes[1].start()

    for which in (1, 0):
        at = slice(FEAT * which, FEAT * which + FEAT)
        for there, i, slot in ((up, 1, 0), (down, 0, 2), (left, 3, 4), (right, 2, 6)):

            def none(slot=slot, at=at):
                rim_in[slot : slot + 2, at] = jnp.zeros((2, FEAT, WIN), BF)

            pl.when(there)(rims(which)[i][1].wait_recv)
            pl.when(jnp.logical_not(there))(none)

        for step in steps:
            pg_copy(which, 0, chip_at(step), chip_at(step), sibling).wait_recv()
        coarse = pg_sum[which, z].astype(F32)
        for step in steps:
            coarse = coarse + pg_in[which, chip_at(step)].astype(F32)
        coarse = (unpack(coarse) * (1.0 / GRP)).T.astype(BF)
        for w in range(4):
            r, c = divmod(w, 2)
            total = g_s[w, at, :WIN] + toward(w ^ 2, r, which) + toward(w ^ 1, 2 + c, which)
            total = total + rim_in[2 * r + c, at].astype(F32)
            total = total + rim_in[4 + 2 * c + r, at].astype(F32)
            row, lane = iota((32, WIN), 0), iota((32, WIN), 1)
            member = jnp.where(row == 8 * w + lane // GRP, 1.0, 0.0).astype(BF)
            total = total + dot(coarse, member)
            (gv_ref if which else gk_ref)[w] = total.astype(BF)
        writes[2 + which].start()

    for which in range(2):
        for there, copies in halos[which]:
            pl.when(there)(lambda copies=copies: wait_sends(copies))
        wait_sends(started[which])
        half_copy(which).wait_send()
        wait_sends(pg_sends(which))
        for there, copy in rims(which):
            pl.when(there)(copy.wait_send)
    share.wait_send()
    for copy in writes:
        copy.wait()


def hand_over(*refs):
    given, out, held, sems = refs[:4], refs[4:8], refs[8:12], refs[12]
    reads = [pltpu.make_async_copy(given[i], held[i], sems.at[i]) for i in range(4)]
    writes = [pltpu.make_async_copy(held[i], out[i], sems.at[4 + i]) for i in range(4)]
    for copy in reads:
        copy.start()
    for read, write in zip(reads, writes):
        read.wait()
        write.start()
    for copy in writes:
        copy.wait()


def local(n_x, n_y, queries, key_field, value_field, grad_output, out_weight, counts, adjacent, far_list):
    def flat(x):
        return x.reshape(4, -1, WIN)

    hbm = pl.BlockSpec(memory_space=pl.ANY)
    shape = jax.ShapeDtypeStruct((4, FEAT, WIN), BF)
    dma = pltpu.SemaphoreType.DMA
    outs = pl.pallas_call(
        lambda *refs: kernel(n_x, n_y, *refs),
        out_shape=[shape] * 4,
        in_specs=[hbm] * 8,
        out_specs=[hbm] * 4,
        scratch_shapes=[
            pltpu.SMEM(counts.shape, jnp.int32),
            pltpu.SMEM(adjacent.shape, jnp.int32),
            pltpu.SMEM(far_list.shape, jnp.int32),
            pltpu.VMEM((4, FEAT, WIN), BF),
            pltpu.VMEM((4, 2 * FEAT, WIN), BF),
            pltpu.VMEM((FEAT, 2 * FEAT), BF),
            pltpu.VMEM((4, FEAT, WIN), BF),
            pltpu.VMEM((4, FEAT, WIN), BF),
            pltpu.VMEM((4, FEAT, WIN), BF),
            pltpu.VMEM((4, FEAT, WIN), BF),
            pltpu.VMEM((12, AUG, WIN), BF),
            pltpu.VMEM((12, FEAT, WIN), BF),
            pltpu.VMEM((4, 4, AUG, WIN), BF),
            pltpu.VMEM((4, 4, FEAT, WIN), BF),
            pltpu.VMEM((4, 512, 256), BF),
            pltpu.VMEM((4, 512, 256), BF),
            pltpu.VMEM((n_y // 2, 2, 48, WIN), BF),
            pltpu.VMEM((n_y // 2, 2, 48, WIN), BF),
            pltpu.VMEM((4, FEAT, WIN), BF),
            pltpu.VMEM((2 * FEAT, FEAT), BF),
            pltpu.VMEM((4, PAIRS, 512, 256), BF),
            pltpu.VMEM((4, PAIRS, 3, 8, 256), F32),
            pltpu.VMEM((4, PAIRS, 3, 80, 256), F32),
            pltpu.VMEM((4, PAIRS, 3, 8, 256), F32),
            pltpu.VMEM((4, PAIRS, 8, 256), F32),
            pltpu.VMEM((4, FEAT, WIN), BF),
            pltpu.VMEM((4, FEAT, WIN), F32),
            pltpu.VMEM((4, 2 * FEAT, 512), F32),
            pltpu.VMEM((2, n_y // 2, 2, 48, WIN), BF),
            pltpu.VMEM((2, n_y // 2, 48, WIN), BF),
            pltpu.VMEM((2, n_y // 2, 48, WIN), BF),
            pltpu.VMEM((2, n_y // 2, 48, WIN), BF),
            pltpu.VMEM((8, 2 * FEAT, WIN), BF),
            pltpu.VMEM((8, 2 * FEAT, WIN), BF),
            pltpu.VMEM((4, FEAT, WIN), BF),
            pltpu.VMEM((4, FEAT, WIN), BF),
            pltpu.VMEM((4, FEAT, WIN), F32),
            dma((12,)),
            dma((12,)),
            dma((2 * n_y,)),
            dma((2 * n_y,)),
            dma((8,)),
            dma((8,)),
            dma((n_y,)),
            dma((n_y,)),
            dma((2,)),
            dma((2,)),
            dma((1,)),
            dma((1,)),
            dma((8,)),
            dma((4,)),
        ],
        compiler_params=pltpu.CompilerParams(
            collective_id=0, has_side_effects=True, vmem_limit_bytes=VMEM
        ),
    )(flat(queries), flat(key_field), flat(value_field), flat(grad_output), out_weight, counts, adjacent, far_list)
    block_out, grad_queries, grad_keys, grad_values = pl.pallas_call(
        hand_over,
        out_shape=[shape] * 4,
        in_specs=[hbm] * 4,
        out_specs=[hbm] * 4,
        scratch_shapes=[pltpu.VMEM((4, FEAT, WIN), BF)] * 4 + [dma((8,))],
        compiler_params=pltpu.CompilerParams(vmem_limit_bytes=VMEM),
    )(*outs)
    return (
        block_out.reshape(2, 2, FEAT, WIN),
        grad_queries.reshape(queries.shape),
        grad_keys.reshape(queries.shape),
        grad_values.reshape(queries.shape),
    )


def solution(mesh):
    n_x, n_y = mesh.shape["sx"], mesh.shape["sy"]
    grid = P("sx", "sy")
    heads = P("sx", "sy", "hd", None, None)
    return jax.shard_map(
        lambda *args: local(n_x, n_y, *args),
        mesh=mesh,
        in_specs=(heads, heads, heads, grid, P("hd", None), grid, grid, grid),
        out_specs=(P("sx", "sy", "hd", None), heads, heads, heads),
        check_vma=False,
    )
```

```python
import math

import jax
import jax.numpy as jnp
from jax import lax
from jax.experimental import pallas as pl
from jax.experimental.pallas import tpu as pltpu
from jax.sharding import PartitionSpec as P

MESH = pl.DeviceIdType.MESH
BF, F32 = jnp.bfloat16, jnp.float32
WIN = 128
DH = 32
FEAT = 192
AUG = 208
PAIRS = 3
GRP = 16
VMEM = 63 * 1024 * 1024
MASKED = -1e30
MARK = 1e4
SCALE = 1.0 / math.sqrt(DH)
EXPC = SCALE * math.log2(math.e)
PARTS = ((0, 1), (1, 3), (3, 4))
NT = (((1,), (1,)), ((), ()))


def dot(a, b):
    return jnp.dot(a, b, preferred_element_type=F32)


def dot_nt(a, b):
    return lax.dot_general(a, b, NT, preferred_element_type=F32)


def iota(shape, dim):
    return lax.broadcasted_iota(jnp.int32, shape, dim)


def diagonal(first, second):
    zero = jnp.zeros_like(first)
    return jnp.concatenate(
        [jnp.concatenate([first, zero], 1), jnp.concatenate([zero, second], 1)], 0
    )


def stacked(*pieces):
    rest = WIN - sum(piece.shape[0] for piece in pieces)
    return jnp.concatenate(list(pieces) + ([jnp.zeros((rest, 256), BF)] if rest else []), 0)


def neighbours(w):
    r, c = divmod(w, 2)
    return (
        w - 2 if r else 4 + c,
        6 + c if r else w + 2,
        w - 1 if c else 8 + r,
        10 + r if c else w + 1,
    )


def pack(x):
    tail = jnp.concatenate([x[:, :16, WIN:], x[:, 16:, WIN:]], 2)
    return jnp.concatenate([x[:, :, :WIN], tail], 1)


def unpack(x):
    tail = jnp.concatenate([x[32:, :64], x[32:, 64:]], 0)
    return jnp.concatenate([x[:32], tail], 1)


def kernel(
    n_x,
    n_y,
    q_in,
    k_in,
    v_in,
    go_in,
    ow_in,
    cnt_in,
    adj_in,
    far_in,
    bo_out_ref,
    gq_out_ref,
    gk_out_ref,
    gv_out_ref,
    cnt_ref,
    adj_ref,
    far_ref,
    q_ref,
    go_ref,
    ow_ref,
    bo_ref,
    gq_ref,
    gk_ref,
    gv_ref,
    kx,
    vx,
    kk,
    vv,
    kt,
    vt,
    pool_k,
    pool_v,
    gm,
    owt,
    e_s,
    m_s,
    a_s,
    f_s,
    c_s,
    att,
    gq_s,
    g_s,
    pg_out,
    pg_half,
    pg_sum,
    pg_in,
    rim_out,
    rim_in,
    bo_out,
    bo_in,
    bo_own,
    halo_send,
    halo_recv,
    pool_send,
    pool_recv,
    rim_send,
    rim_recv,
    pg_send,
    pg_recv,
    half_send,
    half_recv,
    bo_send,
    bo_recv,
    in_sem,
    out_sem,
):
    sx, sy, hd = lax.axis_index("sx"), lax.axis_index("sy"), lax.axis_index("hd")
    up, down = sx > 0, sx < n_x - 1
    left, right = sy > 0, sy < n_y - 1
    x_lo, x_hi = {"sx": jnp.maximum(sx - 1, 0)}, {"sx": jnp.minimum(sx + 1, n_x - 1)}
    y_lo, y_hi = {"sy": jnp.maximum(sy - 1, 0)}, {"sy": jnp.minimum(sy + 1, n_y - 1)}
    n_z = n_y // 2
    z, core = sy // 2, lax.rem(sy, 2)
    sibling = {"sy": sy + 1 - 2 * core}
    outer = {"sy": lax.rem(sy + 2 * core - 1 + n_y, n_y)}
    partner = {"hd": 1 - hd}

    def chip_at(step):
        return lax.rem(z + step + n_z, n_z)

    barrier = pltpu.get_barrier_semaphore()

    def greet(where):
        pl.semaphore_signal(barrier, inc=1, device_id=where, device_id_type=MESH)

    steps = sorted(range(1, n_z), key=lambda step: -min(step, n_z - step))
    others = [chip_at(step) for step in steps]
    for chip in others:
        greet({"sy": 2 * chip + core})
    pl.when(up)(lambda: greet(x_lo))
    pl.when(down)(lambda: greet(x_hi))
    for where in (partner, outer, sibling):
        greet(where)

    reads = [
        pltpu.make_async_copy(src, dst, in_sem.at[i])
        for i, (src, dst) in enumerate(
            (
                (k_in, kx.at[pl.ds(0, 4), pl.ds(0, FEAT)]),
                (v_in, vx.at[pl.ds(0, 4)]),
                (cnt_in, cnt_ref),
                (go_in, go_ref),
                (ow_in, ow_ref),
                (q_in, q_ref),
                (adj_in, adj_ref),
                (far_in, far_ref),
            )
        )
    ]
    for copy in reads:
        copy.start()

    for copy in reads[:3]:
        copy.wait()
    pooled_k = pooled_v = None
    for w in range(4):
        r, c = divmod(w, 2)
        keep = GRP * cnt_ref[r, c]
        off = (iota((16, WIN), 0) == 0) & (iota((16, WIN), 1) >= keep)
        kx[w, FEAT:AUG] = jnp.where(off, MASKED, 0.0).astype(BF)
        row, lane = iota((32, WIN), 0), iota((32, WIN), 1)
        member = jnp.where(row == 8 * w + lane // GRP, 1.0, 0.0).astype(BF)
        row, lane = iota((32, FEAT), 0), iota((32, FEAT), 1)
        bad = (lane == 0) & (row >= 8 * w + cnt_ref[r, c]) & (row < 8 * w + 8)
        part = dot_nt(member, kx[w, 0:FEAT]) * (1.0 / GRP)
        part = jnp.where(bad, MARK, part)
        pooled_k = part if pooled_k is None else pooled_k + part
        part = dot_nt(member, vx[w]) * (1.0 / GRP)
        pooled_v = part if pooled_v is None else pooled_v + part
    pool_k[z, core] = pack(pooled_k[None])[0].astype(BF)
    pool_v[z, core] = pack(pooled_v[None])[0].astype(BF)

    pl.semaphore_wait(barrier, n_z + 2 + up.astype(jnp.int32) + down.astype(jnp.int32))

    def remote(src, dst, sends, recvs, i, j, where):
        return pltpu.make_async_remote_copy(
            src_ref=src,
            dst_ref=dst,
            send_sem=sends.at[i],
            recv_sem=recvs.at[j],
            device_id=where,
            device_id_type=MESH,
        )

    def start_all(copies):
        for copy in copies:
            copy.start()

    def wait_sends(copies):
        for copy in copies:
            copy.wait_send()

    def wait_recvs(copies):
        for copy in copies:
            copy.wait_recv()

    def halo_copies(ref, base):
        def halo(src, dst, i, where):
            return remote(ref.at[src], ref.at[dst], halo_send, halo_recv, base + i, base + i, where)

        return (
            (up, [halo(pl.ds(0, 2), pl.ds(6, 2), 0, x_lo)]),
            (down, [halo(pl.ds(2, 2), pl.ds(4, 2), 1, x_hi)]),
            (left, [halo(0, 10, 2, y_lo), halo(2, 11, 3, y_lo)]),
            (right, [halo(1, 8, 4, y_hi), halo(3, 9, 5, y_hi)]),
        )

    halos = [halo_copies(kx, 0), halo_copies(vx, 6)]

    def start_halos(which):
        for there, copies in halos[which]:
            pl.when(there)(lambda copies=copies: start_all(copies))

    def halos_arrive(which, ref, fill):
        flat = [copy for _, copies in halos[which] for copy in copies]
        for there, index, slot in ((up, [1], 4), (down, [0], 6), (left, [4, 5], 8), (right, [2, 3], 10)):

            def arrive(index=index):
                wait_recvs([flat[i] for i in index])

            def outside(slot=slot):
                ref[slot : slot + 2] = fill

            pl.when(there)(arrive)
            pl.when(jnp.logical_not(there))(outside)

    pools = (pool_k, pool_v)
    started = ([], [])

    def pooled_copy(which, chip, part, i, where):
        block = pools[which].at[chip, part]
        base = n_y * which
        return remote(block, block, pool_send, pool_recv, base + i, base + 2 * chip + part, where)

    def send_pooled(which, chip, where):
        copy = pooled_copy(which, chip, core, len(started[which]), where)
        copy.start()
        started[which].append(copy)

    def pass_on(which):
        for chip in reversed(others):
            pooled_copy(which, chip, core, 0, sibling).wait_recv()
            send_pooled(which, chip, sibling)

    def handed(which):
        for chip in [z] + others:
            pooled_copy(which, chip, 1 - core, 0, sibling).wait_recv()

    for which in range(2):
        for chip in others:
            send_pooled(which, z, {"sy": 2 * chip + core})
        start_halos(which)
    for which in range(2):
        send_pooled(which, z, sibling)

    def turn_keys(w, b, block):
        pad = jnp.zeros((48, WIN), BF)
        for p in range(PAIRS):
            rows = jnp.concatenate([block[64 * p : 64 * p + 64], block[FEAT:], pad], 0)
            kt[w, p, pl.ds(WIN * b, WIN), :] = rows.T

    def turn_values(w, b, block):
        pad = jnp.zeros((64, WIN), BF)
        vt[w, 0, pl.ds(WIN * b, WIN), :] = block[:WIN].T
        vt[w, 1, pl.ds(WIN * b, WIN), :] = jnp.concatenate([block[WIN:], pad], 0).T

    for copy in reads[3:]:
        copy.wait()
    for w in range(4):
        kk[w, 0] = kx[w]
        vv[w, 0] = vx[w]
        turn_keys(w, 0, kx[w])
        turn_values(w, 0, vx[w])

    def rows_of(ref, w, part, p):
        first, last = PARTS[part]
        return jnp.concatenate(
            [ref[w, b, 64 * p : 64 * p + 64, :] for b in range(first, last)], 1
        )

    def span(part):
        first, last = PARTS[part]
        return slice(WIN * first, WIN * last)

    every = [(w, p) for w in range(4) for p in range(PAIRS)]

    def head(ref, w, h):
        return ref[w, 32 * h : 32 * h + 32, :]

    def score(part):
        one_row = jnp.where(iota((16, 256), 0) == 0, 1.0, 0.0).astype(BF)
        at = span(part)
        for w in range(4):
            pairs = [diagonal(head(q_ref, w, 2 * p), head(q_ref, w, 2 * p + 1)) for p in range(PAIRS)]
            scores = [dot(kt[w, p, at, :], stacked(pairs[p], one_row)) for p in range(PAIRS)]
            tops = [jnp.max(x, axis=0, keepdims=True) for x in scores]
            lows = [jnp.exp2((x - top) * EXPC).astype(BF) for x, top in zip(scores, tops)]
            for p in range(PAIRS):
                e_s[w, p, at, :] = lows[p]
                m_s[w, p, part] = jnp.broadcast_to(tops[p], (8, 256))

    def weigh(part):
        ones = jnp.ones((16, WIN * (PARTS[part][1] - PARTS[part][0])), BF)
        for w, p in every:
            rows = jnp.concatenate([rows_of(vv, w, part, p), ones], 0)
            a_s[w, p, part] = dot(rows, e_s[w, p, span(part), :])

    score(0)
    weigh(0)

    for w in range(4):
        r, c = divmod(w, 2)
        mixed = dot(ow_ref[...], go_ref[w])
        mixed = jnp.where(iota((FEAT, WIN), 1) < GRP * cnt_ref[r, c], mixed, 0.0)
        gm[w] = mixed.astype(BF)
    owt[...] = ow_ref[...].T

    def beside_slot(w, s):
        r, c = divmod(w, 2)
        n0, n1, n2, n3 = neighbours(w)
        code = adj_ref[r, c, s]
        return jnp.where(code < 2, jnp.where(code == 0, n0, n1), jnp.where(code == 2, n2, n3))

    def listed(which, w):
        r, c = divmod(w, 2)
        far = [far_ref[r, c, f] for f in range(4)]
        return jnp.concatenate([unpack(pools[which][e // 2, e % 2]) for e in far], 0).T

    pass_on(0)
    halos_arrive(0, kx, jnp.where(iota((2, AUG, WIN), 1) == FEAT, MASKED, 0.0).astype(BF))
    for w in range(4):
        for s in range(2):
            block = kx[beside_slot(w, s)]
            kk[w, 1 + s] = block
            turn_keys(w, 1 + s, block)
    score(1)

    handed(0)
    for w in range(4):
        rows = listed(0, w)
        bad = (iota((16, WIN), 0) == 0) & (rows[:16].astype(F32) > 0.5 * MARK)
        block = jnp.concatenate([rows, jnp.where(bad, MASKED, 0.0).astype(BF)], 0)
        kk[w, 3] = block
        turn_keys(w, 3, block)
    pass_on(1)
    score(2)

    halos_arrive(1, vx, jnp.zeros((2, FEAT, WIN), BF))
    for w in range(4):
        for s in range(2):
            block = vx[beside_slot(w, s)]
            vv[w, 1 + s] = block
            turn_values(w, 1 + s, block)
    weigh(1)
    handed(1)
    for w in range(4):
        block = listed(1, w)
        vv[w, 3] = block
        turn_values(w, 3, block)
    weigh(2)

    for w, p in every:
        keep = GRP * cnt_ref[w // 2, w % 2]
        tops = [m_s[w, p, i, 0:1, :] for i in range(3)]
        top = jnp.maximum(jnp.maximum(tops[0], tops[1]), tops[2])
        shares = [jnp.exp2((t - top) * EXPC) for t in tops]
        total = sum(share * a_s[w, p, i] for i, share in enumerate(shares))
        inverse = 1.0 / total[64:65]
        first = total[:32, :WIN] * inverse[:, :WIN]
        second = total[32:64, WIN:] * inverse[:, WIN:]
        both = jnp.concatenate([first, second], 0)
        product = both * gm[w, 64 * p : 64 * p + 64, :].astype(F32)
        centre = jnp.concatenate(
            [
                jnp.sum(product[:32], axis=0, keepdims=True),
                jnp.sum(product[32:], axis=0, keepdims=True),
            ],
            1,
        )
        c_s[w, p] = jnp.broadcast_to(centre, (8, 256))
        for i, share in enumerate(shares):
            f_s[w, p, i] = jnp.broadcast_to(share * inverse, (8, 256))
        both = jnp.where(iota((64, WIN), 1) < keep, both, 0.0)
        att[w, 64 * p : 64 * p + 64, :] = both.astype(BF)

    def scaled_heads(ref, w, p, factor):
        return diagonal(
            (head(ref, w, 2 * p).astype(F32) * factor[:, :WIN]).astype(BF),
            (head(ref, w, 2 * p + 1).astype(F32) * factor[:, WIN:]).astype(BF),
        )

    def value_terms(part):
        at = span(part)
        for w, p in every:
            rows = scaled_heads(gm, w, p, f_s[w, p, part, 0:1, :])
            g_s[w, FEAT + 64 * p : FEAT + 64 * p + 64, at] = dot_nt(rows, e_s[w, p, at, :])

    def key_terms(part):
        no_rows = jnp.zeros((64, 256), BF)
        at = span(part)
        for w in range(4):
            slopes, backs, terms = [], [], []
            lows = [e_s[w, p, at, :] for p in range(PAIRS)]
            olds = [gq_s[w, 64 * p : 64 * p + 64, :] for p in range(PAIRS)]
            for p in range(PAIRS):
                pair = diagonal(head(gm, w, 2 * p), head(gm, w, 2 * p + 1))
                pair = stacked(no_rows, pair) if p % 2 else stacked(pair)
                prob = dot(vt[w, p // 2, at, :], pair)
                slopes.append((lows[p].astype(F32) * (prob - c_s[w, p, 0:1, :])).astype(BF))
            for p in range(PAIRS):
                scaled = f_s[w, p, part, 0:1, :] * SCALE
                back = dot(rows_of(kk, w, part, p), slopes[p]) * scaled
                backs.append(jnp.concatenate([back[:32, :WIN], back[32:, WIN:]], 0))
                terms.append(dot_nt(scaled_heads(q_ref, w, p, scaled), slopes[p]))
            for p in range(PAIRS):
                rows = slice(64 * p, 64 * p + 64)
                back = backs[p] if part == 1 else backs[p] + olds[p]
                if part == 0:
                    gq_ref[w, rows, :] = back.astype(BF)
                else:
                    gq_s[w, rows, :] = back
                g_s[w, rows, at] = terms[p]

    entries = 32 * n_y
    chosen = []
    for w in range(4):
        row, lane = iota((entries, WIN), 0), iota((entries, WIN), 1)
        want = jnp.zeros((entries, WIN), jnp.int32)
        for f in range(4):
            code = far_ref[w // 2, w % 2, f]
            want = jnp.where(lane // 32 == f, 32 * code + lane - 32 * f, want)
        chosen.append(jnp.where(row == want, 1.0, 0.0).astype(BF))

    def half_copy(which):
        return remote(
            pg_out.at[which, :, 1 - core], pg_half.at[which], half_send, half_recv, which, which, sibling
        )

    def send_half(which):
        spread = None
        for w in range(4):
            term = dot_nt(chosen[w], g_s[w, FEAT * which : FEAT * which + FEAT, 3 * WIN :].astype(BF))
            spread = term if spread is None else spread + term
        spread = pack(spread.reshape(n_y, 32, FEAT)).astype(BF)
        pg_out[which] = spread.reshape(n_z, 2, 48, WIN)
        half_copy(which).start()

    def pg_copy(which, i, src, dst, where):
        i, j = n_z * which + i, n_z * which + dst
        return remote(pg_sum.at[which, src], pg_in.at[which, dst], pg_send, pg_recv, i, j, where)

    def pg_sends(which):
        return [
            pg_copy(which, i, chip_at(step), z, {"sy": 2 * chip_at(step) + core})
            for i, step in enumerate(steps)
        ]

    def send_owners(which):
        half_copy(which).wait_recv()
        both = pg_out[which, :, core].astype(F32) + pg_half[which].astype(F32)
        pg_sum[which] = both.astype(BF)
        start_all(pg_sends(which))

    def toward(w, code, which):
        r, c = divmod(w, 2)
        total = None
        for s in range(2):
            here = (adj_ref[r, c, s] == code).astype(F32)
            term = g_s[w, FEAT * which : FEAT * which + FEAT, (1 + s) * WIN : (2 + s) * WIN] * here
            total = term if total is None else total + term
        return total

    def rims(which):
        def rim(src, dst, i, where):
            rows = pl.ds(FEAT * which, FEAT)
            i = 4 * which + i
            return remote(
                rim_out.at[pl.ds(src, 2), rows],
                rim_in.at[pl.ds(dst, 2), rows],
                rim_send,
                rim_recv,
                i,
                i,
                where,
            )

        return (
            (up, rim(0, 2, 0, x_lo)),
            (down, rim(2, 0, 1, x_hi)),
            (left, rim(4, 6, 2, y_lo)),
            (right, rim(6, 4, 3, y_hi)),
        )

    def send_rims(which):
        at = slice(FEAT * which, FEAT * which + FEAT)
        for w in range(4):
            r, c = divmod(w, 2)
            rim_out[2 * r + c, at] = toward(w, r, which).astype(BF)
            rim_out[4 + 2 * c + r, at] = toward(w, 2 + c, which).astype(BF)
        for there, copy in rims(which):
            pl.when(there)(copy.start)

    mine = pl.ds(pl.multiple_of(hd * FEAT, FEAT), FEAT)
    theirs = pl.ds(pl.multiple_of((1 - hd) * FEAT, FEAT), FEAT)
    for w in range(4):
        bo_out[w] = dot(owt[theirs, :], att[w]).astype(BF)
    share = remote(bo_out, bo_in, bo_send, bo_recv, 0, 0, partner)
    share.start()

    value_terms(2)
    send_half(1)
    value_terms(1)
    send_rims(1)
    send_owners(1)
    key_terms(1)
    send_rims(0)
    key_terms(2)
    send_half(0)
    value_terms(0)
    send_owners(0)
    key_terms(0)

    writes = [
        pltpu.make_async_copy(src, dst, out_sem.at[i])
        for i, (src, dst) in enumerate(
            ((gq_ref, gq_out_ref), (bo_ref, bo_out_ref), (gk_ref, gk_out_ref), (gv_ref, gv_out_ref))
        )
    ]
    writes[0].start()

    for w in range(4):
        bo_own[w] = dot(owt[mine, :], att[w])

    share.wait_recv()
    for w in range(4):
        bo_ref[w] = (bo_own[w] + bo_in[w].astype(F32)).astype(BF)
    writes[1].start()

    for which in (1, 0):
        at = slice(FEAT * which, FEAT * which + FEAT)
        for there, i, slot in ((up, 1, 0), (down, 0, 2), (left, 3, 4), (right, 2, 6)):

            def none(slot=slot, at=at):
                rim_in[slot : slot + 2, at] = jnp.zeros((2, FEAT, WIN), BF)

            pl.when(there)(rims(which)[i][1].wait_recv)
            pl.when(jnp.logical_not(there))(none)

        for step in steps:
            pg_copy(which, 0, chip_at(step), chip_at(step), sibling).wait_recv()
        coarse = pg_sum[which, z].astype(F32)
        for step in steps:
            coarse = coarse + pg_in[which, chip_at(step)].astype(F32)
        coarse = (unpack(coarse) * (1.0 / GRP)).T.astype(BF)
        for w in range(4):
            r, c = divmod(w, 2)
            total = g_s[w, at, :WIN] + toward(w ^ 2, r, which) + toward(w ^ 1, 2 + c, which)
            total = total + rim_in[2 * r + c, at].astype(F32)
            total = total + rim_in[4 + 2 * c + r, at].astype(F32)
            row, lane = iota((32, WIN), 0), iota((32, WIN), 1)
            member = jnp.where(row == 8 * w + lane // GRP, 1.0, 0.0).astype(BF)
            total = total + dot(coarse, member)
            (gv_ref if which else gk_ref)[w] = total.astype(BF)
        writes[2 + which].start()

    for which in range(2):
        for there, copies in halos[which]:
            pl.when(there)(lambda copies=copies: wait_sends(copies))
        wait_sends(started[which])
        half_copy(which).wait_send()
        wait_sends(pg_sends(which))
        for there, copy in rims(which):
            pl.when(there)(copy.wait_send)
    share.wait_send()
    for copy in writes:
        copy.wait()


def hand_over(*refs):
    given, out, held, sems = refs[:4], refs[4:8], refs[8:12], refs[12]
    reads = [pltpu.make_async_copy(given[i], held[i], sems.at[i]) for i in range(4)]
    writes = [pltpu.make_async_copy(held[i], out[i], sems.at[4 + i]) for i in range(4)]
    for copy in reads:
        copy.start()
    for read, write in zip(reads, writes):
        read.wait()
        write.start()
    for copy in writes:
        copy.wait()


def local(n_x, n_y, queries, key_field, value_field, grad_output, out_weight, counts, adjacent, far_list):
    def flat(x):
        return x.reshape(4, -1, WIN)

    hbm = pl.BlockSpec(memory_space=pl.ANY)
    shape = jax.ShapeDtypeStruct((4, FEAT, WIN), BF)
    dma = pltpu.SemaphoreType.DMA
    outs = pl.pallas_call(
        lambda *refs: kernel(n_x, n_y, *refs),
        out_shape=[shape] * 4,
        in_specs=[hbm] * 8,
        out_specs=[hbm] * 4,
        scratch_shapes=[
            pltpu.SMEM(counts.shape, jnp.int32),
            pltpu.SMEM(adjacent.shape, jnp.int32),
            pltpu.SMEM(far_list.shape, jnp.int32),
            pltpu.VMEM((4, FEAT, WIN), BF),
            pltpu.VMEM((4, 2 * FEAT, WIN), BF),
            pltpu.VMEM((FEAT, 2 * FEAT), BF),
            pltpu.VMEM((4, FEAT, WIN), BF),
            pltpu.VMEM((4, FEAT, WIN), BF),
            pltpu.VMEM((4, FEAT, WIN), BF),
            pltpu.VMEM((4, FEAT, WIN), BF),
            pltpu.VMEM((12, AUG, WIN), BF),
            pltpu.VMEM((12, FEAT, WIN), BF),
            pltpu.VMEM((4, 4, AUG, WIN), BF),
            pltpu.VMEM((4, 4, FEAT, WIN), BF),
            pltpu.VMEM((4, PAIRS, 512, WIN), BF),
            pltpu.VMEM((4, 2, 512, WIN), BF),
            pltpu.VMEM((n_y // 2, 2, 48, WIN), BF),
            pltpu.VMEM((n_y // 2, 2, 48, WIN), BF),
            pltpu.VMEM((4, FEAT, WIN), BF),
            pltpu.VMEM((2 * FEAT, FEAT), BF),
            pltpu.VMEM((4, PAIRS, 512, 256), BF),
            pltpu.VMEM((4, PAIRS, 3, 8, 256), F32),
            pltpu.VMEM((4, PAIRS, 3, 80, 256), F32),
            pltpu.VMEM((4, PAIRS, 3, 8, 256), F32),
            pltpu.VMEM((4, PAIRS, 8, 256), F32),
            pltpu.VMEM((4, FEAT, WIN), BF),
            pltpu.VMEM((4, FEAT, WIN), F32),
            pltpu.VMEM((4, 2 * FEAT, 512), F32),
            pltpu.VMEM((2, n_y // 2, 2, 48, WIN), BF),
            pltpu.VMEM((2, n_y // 2, 48, WIN), BF),
            pltpu.VMEM((2, n_y // 2, 48, WIN), BF),
            pltpu.VMEM((2, n_y // 2, 48, WIN), BF),
            pltpu.VMEM((8, 2 * FEAT, WIN), BF),
            pltpu.VMEM((8, 2 * FEAT, WIN), BF),
            pltpu.VMEM((4, FEAT, WIN), BF),
            pltpu.VMEM((4, FEAT, WIN), BF),
            pltpu.VMEM((4, FEAT, WIN), F32),
            dma((12,)),
            dma((12,)),
            dma((2 * n_y,)),
            dma((2 * n_y,)),
            dma((8,)),
            dma((8,)),
            dma((n_y,)),
            dma((n_y,)),
            dma((2,)),
            dma((2,)),
            dma((1,)),
            dma((1,)),
            dma((8,)),
            dma((4,)),
        ],
        compiler_params=pltpu.CompilerParams(
            collective_id=0, has_side_effects=True, vmem_limit_bytes=VMEM
        ),
    )(flat(queries), flat(key_field), flat(value_field), flat(grad_output), out_weight, counts, adjacent, far_list)
    block_out, grad_queries, grad_keys, grad_values = pl.pallas_call(
        hand_over,
        out_shape=[shape] * 4,
        in_specs=[hbm] * 4,
        out_specs=[hbm] * 4,
        scratch_shapes=[pltpu.VMEM((4, FEAT, WIN), BF)] * 4 + [dma((8,))],
        compiler_params=pltpu.CompilerParams(vmem_limit_bytes=VMEM),
    )(*outs)
    return (
        block_out.reshape(2, 2, FEAT, WIN),
        grad_queries.reshape(queries.shape),
        grad_keys.reshape(queries.shape),
        grad_values.reshape(queries.shape),
    )


def solution(mesh):
    n_x, n_y = mesh.shape["sx"], mesh.shape["sy"]
    grid = P("sx", "sy")
    heads = P("sx", "sy", "hd", None, None)
    return jax.shard_map(
        lambda *args: local(n_x, n_y, *args),
        mesh=mesh,
        in_specs=(heads, heads, heads, grid, P("hd", None), grid, grid, grid),
        out_specs=(P("sx", "sy", "hd", None), heads, heads, heads),
        check_vma=False,
    )
```

```python
import math

import jax
import jax.numpy as jnp
from jax import lax
from jax.experimental import pallas as pl
from jax.experimental.pallas import tpu as pltpu
from jax.sharding import PartitionSpec as P

MESH = pl.DeviceIdType.MESH
BF, F32 = jnp.bfloat16, jnp.float32
WIN = 128
DH = 32
FEAT = 192
AUG = 208
PAIRS = 3
GRP = 16
VMEM = 63 * 1024 * 1024
MASKED = -1e30
MARK = 1e4
SCALE = 1.0 / math.sqrt(DH)
EXPC = SCALE * math.log2(math.e)
PARTS = ((0, 1), (1, 3), (3, 4))
NT = (((1,), (1,)), ((), ()))


def dot(a, b):
    return jnp.dot(a, b, preferred_element_type=F32)


def dot_nt(a, b):
    return lax.dot_general(a, b, NT, preferred_element_type=F32)


def iota(shape, dim):
    return lax.broadcasted_iota(jnp.int32, shape, dim)


def diagonal(first, second):
    zero = jnp.zeros_like(first)
    return jnp.concatenate(
        [jnp.concatenate([first, zero], 1), jnp.concatenate([zero, second], 1)], 0
    )


def stacked(*pieces):
    rest = WIN - sum(piece.shape[0] for piece in pieces)
    return jnp.concatenate(list(pieces) + ([jnp.zeros((rest, 256), BF)] if rest else []), 0)


def neighbours(w):
    r, c = divmod(w, 2)
    return (
        w - 2 if r else 4 + c,
        6 + c if r else w + 2,
        w - 1 if c else 8 + r,
        10 + r if c else w + 1,
    )


def pack(x):
    tail = jnp.concatenate([x[:, :16, WIN:], x[:, 16:, WIN:]], 2)
    return jnp.concatenate([x[:, :, :WIN], tail], 1)


def unpack(x):
    tail = jnp.concatenate([x[32:, :64], x[32:, 64:]], 0)
    return jnp.concatenate([x[:32], tail], 1)


def kernel(
    n_x,
    n_y,
    q_in,
    k_in,
    v_in,
    go_in,
    ow_in,
    cnt_in,
    adj_in,
    far_in,
    bo_out_ref,
    gq_out_ref,
    gk_out_ref,
    gv_out_ref,
    cnt_ref,
    adj_ref,
    far_ref,
    q_ref,
    go_ref,
    ow_ref,
    bo_ref,
    gq_ref,
    gk_ref,
    gv_ref,
    kx,
    vx,
    kk,
    vv,
    kt,
    vt,
    pool_k,
    pool_v,
    gm,
    owt,
    e_s,
    prob_s,
    m_s,
    a_s,
    f_s,
    c_s,
    att,
    gq_s,
    g_s,
    pg_out,
    pg_half,
    pg_sum,
    pg_in,
    rim_out,
    rim_in,
    bo_out,
    bo_in,
    bo_own,
    halo_send,
    halo_recv,
    pool_send,
    pool_recv,
    rim_send,
    rim_recv,
    pg_send,
    pg_recv,
    half_send,
    half_recv,
    bo_send,
    bo_recv,
    in_sem,
    out_sem,
):
    sx, sy, hd = lax.axis_index("sx"), lax.axis_index("sy"), lax.axis_index("hd")
    up, down = sx > 0, sx < n_x - 1
    left, right = sy > 0, sy < n_y - 1
    x_lo, x_hi = {"sx": jnp.maximum(sx - 1, 0)}, {"sx": jnp.minimum(sx + 1, n_x - 1)}
    y_lo, y_hi = {"sy": jnp.maximum(sy - 1, 0)}, {"sy": jnp.minimum(sy + 1, n_y - 1)}
    n_z = n_y // 2
    z, core = sy // 2, lax.rem(sy, 2)
    sibling = {"sy": sy + 1 - 2 * core}
    outer = {"sy": lax.rem(sy + 2 * core - 1 + n_y, n_y)}
    partner = {"hd": 1 - hd}

    def chip_at(step):
        return lax.rem(z + step + n_z, n_z)

    barrier = pltpu.get_barrier_semaphore()

    def greet(where):
        pl.semaphore_signal(barrier, inc=1, device_id=where, device_id_type=MESH)

    steps = sorted(range(1, n_z), key=lambda step: -min(step, n_z - step))
    others = [chip_at(step) for step in steps]
    for chip in others:
        greet({"sy": 2 * chip + core})
    pl.when(up)(lambda: greet(x_lo))
    pl.when(down)(lambda: greet(x_hi))
    for where in (partner, outer, sibling):
        greet(where)

    reads = [
        pltpu.make_async_copy(src, dst, in_sem.at[i])
        for i, (src, dst) in enumerate(
            (
                (k_in, kx.at[pl.ds(0, 4), pl.ds(0, FEAT)]),
                (v_in, vx.at[pl.ds(0, 4)]),
                (cnt_in, cnt_ref),
                (go_in, go_ref),
                (ow_in, ow_ref),
                (q_in, q_ref),
                (adj_in, adj_ref),
                (far_in, far_ref),
            )
        )
    ]
    for copy in reads:
        copy.start()

    for copy in reads[:3]:
        copy.wait()
    pooled_k = pooled_v = None
    for w in range(4):
        r, c = divmod(w, 2)
        keep = GRP * cnt_ref[r, c]
        off = (iota((16, WIN), 0) == 0) & (iota((16, WIN), 1) >= keep)
        kx[w, FEAT:AUG] = jnp.where(off, MASKED, 0.0).astype(BF)
        row, lane = iota((32, WIN), 0), iota((32, WIN), 1)
        member = jnp.where(row == 8 * w + lane // GRP, 1.0, 0.0).astype(BF)
        row, lane = iota((32, FEAT), 0), iota((32, FEAT), 1)
        bad = (lane == 0) & (row >= 8 * w + cnt_ref[r, c]) & (row < 8 * w + 8)
        part = dot_nt(member, kx[w, 0:FEAT]) * (1.0 / GRP)
        part = jnp.where(bad, MARK, part)
        pooled_k = part if pooled_k is None else pooled_k + part
        part = dot_nt(member, vx[w]) * (1.0 / GRP)
        pooled_v = part if pooled_v is None else pooled_v + part
    pool_k[z, core] = pack(pooled_k[None])[0].astype(BF)
    pool_v[z, core] = pack(pooled_v[None])[0].astype(BF)

    pl.semaphore_wait(barrier, n_z + 2 + up.astype(jnp.int32) + down.astype(jnp.int32))

    def remote(src, dst, sends, recvs, i, j, where):
        return pltpu.make_async_remote_copy(
            src_ref=src,
            dst_ref=dst,
            send_sem=sends.at[i],
            recv_sem=recvs.at[j],
            device_id=where,
            device_id_type=MESH,
        )

    def start_all(copies):
        for copy in copies:
            copy.start()

    def wait_sends(copies):
        for copy in copies:
            copy.wait_send()

    def wait_recvs(copies):
        for copy in copies:
            copy.wait_recv()

    def halo_copies(ref, base):
        def halo(src, dst, i, where):
            return remote(ref.at[src], ref.at[dst], halo_send, halo_recv, base + i, base + i, where)

        return (
            (up, [halo(pl.ds(0, 2), pl.ds(6, 2), 0, x_lo)]),
            (down, [halo(pl.ds(2, 2), pl.ds(4, 2), 1, x_hi)]),
            (left, [halo(0, 10, 2, y_lo), halo(2, 11, 3, y_lo)]),
            (right, [halo(1, 8, 4, y_hi), halo(3, 9, 5, y_hi)]),
        )

    halos = [halo_copies(kx, 0), halo_copies(vx, 6)]

    def start_halos(which):
        for there, copies in halos[which]:
            pl.when(there)(lambda copies=copies: start_all(copies))

    def halos_arrive(which, ref, fill):
        flat = [copy for _, copies in halos[which] for copy in copies]
        for there, index, slot in ((up, [1], 4), (down, [0], 6), (left, [4, 5], 8), (right, [2, 3], 10)):

            def arrive(index=index):
                wait_recvs([flat[i] for i in index])

            def outside(slot=slot):
                ref[slot : slot + 2] = fill

            pl.when(there)(arrive)
            pl.when(jnp.logical_not(there))(outside)

    pools = (pool_k, pool_v)
    started = ([], [])

    def pooled_copy(which, chip, part, i, where):
        block = pools[which].at[chip, part]
        base = n_y * which
        return remote(block, block, pool_send, pool_recv, base + i, base + 2 * chip + part, where)

    def send_pooled(which, chip, where):
        copy = pooled_copy(which, chip, core, len(started[which]), where)
        copy.start()
        started[which].append(copy)

    def pass_on(which):
        for chip in reversed(others):
            pooled_copy(which, chip, core, 0, sibling).wait_recv()
            send_pooled(which, chip, sibling)

    def handed(which):
        for chip in [z] + others:
            pooled_copy(which, chip, 1 - core, 0, sibling).wait_recv()

    for which in range(2):
        for chip in others:
            send_pooled(which, z, {"sy": 2 * chip + core})
        start_halos(which)
    for which in range(2):
        send_pooled(which, z, sibling)

    def turn_keys(w, b, block):
        pad = jnp.zeros((48, WIN), BF)
        for p in range(PAIRS):
            rows = jnp.concatenate([block[64 * p : 64 * p + 64], block[FEAT:], pad], 0)
            kt[w, p, pl.ds(WIN * b, WIN), :] = rows.T

    def turn_values(w, b, block):
        pad = jnp.zeros((64, WIN), BF)
        vt[w, 0, pl.ds(WIN * b, WIN), :] = block[:WIN].T
        vt[w, 1, pl.ds(WIN * b, WIN), :] = jnp.concatenate([block[WIN:], pad], 0).T

    for copy in reads[3:]:
        copy.wait()
    for w in range(4):
        kk[w, 0] = kx[w]
        vv[w, 0] = vx[w]
        turn_keys(w, 0, kx[w])
        turn_values(w, 0, vx[w])

    def rows_of(ref, w, part, p):
        first, last = PARTS[part]
        return jnp.concatenate(
            [ref[w, b, 64 * p : 64 * p + 64, :] for b in range(first, last)], 1
        )

    def span(part):
        first, last = PARTS[part]
        return slice(WIN * first, WIN * last)

    every = [(w, p) for w in range(4) for p in range(PAIRS)]

    def head(ref, w, h):
        return ref[w, 32 * h : 32 * h + 32, :]

    def score(part):
        one_row = jnp.where(iota((16, 256), 0) == 0, 1.0, 0.0).astype(BF)
        at = span(part)
        for w in range(4):
            pairs = [diagonal(head(q_ref, w, 2 * p), head(q_ref, w, 2 * p + 1)) for p in range(PAIRS)]
            scores = [dot(kt[w, p, at, :], stacked(pairs[p], one_row)) for p in range(PAIRS)]
            tops = [jnp.max(x, axis=0, keepdims=True) for x in scores]
            lows = [jnp.exp2((x - top) * EXPC).astype(BF) for x, top in zip(scores, tops)]
            for p in range(PAIRS):
                e_s[w, p, at, :] = lows[p]
                m_s[w, p, part] = jnp.broadcast_to(tops[p], (8, 256))

    def weigh(part):
        ones = jnp.ones((16, WIN * (PARTS[part][1] - PARTS[part][0])), BF)
        for w, p in every:
            rows = jnp.concatenate([rows_of(vv, w, part, p), ones], 0)
            a_s[w, p, part] = dot(rows, e_s[w, p, span(part), :])

    def grad_prob(w, p, at):
        pair = diagonal(head(gm, w, 2 * p), head(gm, w, 2 * p + 1))
        pair = stacked(jnp.zeros((64, 256), BF), pair) if p % 2 else stacked(pair)
        return dot(vt[w, p // 2, at, :], pair)

    def keep_prob(part):
        for w, p in every:
            prob_s[w, p, span(part), :] = grad_prob(w, p, span(part))

    score(0)
    weigh(0)

    for w in range(4):
        r, c = divmod(w, 2)
        mixed = dot(ow_ref[...], go_ref[w])
        mixed = jnp.where(iota((FEAT, WIN), 1) < GRP * cnt_ref[r, c], mixed, 0.0)
        gm[w] = mixed.astype(BF)
    owt[...] = ow_ref[...].T

    def beside_slot(w, s):
        r, c = divmod(w, 2)
        n0, n1, n2, n3 = neighbours(w)
        code = adj_ref[r, c, s]
        return jnp.where(code < 2, jnp.where(code == 0, n0, n1), jnp.where(code == 2, n2, n3))

    def listed(which, w):
        r, c = divmod(w, 2)
        far = [far_ref[r, c, f] for f in range(4)]
        return jnp.concatenate([unpack(pools[which][e // 2, e % 2]) for e in far], 0).T

    keep_prob(0)
    pass_on(0)
    halos_arrive(0, kx, jnp.where(iota((2, AUG, WIN), 1) == FEAT, MASKED, 0.0).astype(BF))
    for w in range(4):
        for s in range(2):
            block = kx[beside_slot(w, s)]
            kk[w, 1 + s] = block
            turn_keys(w, 1 + s, block)
    score(1)

    handed(0)
    for w in range(4):
        rows = listed(0, w)
        bad = (iota((16, WIN), 0) == 0) & (rows[:16].astype(F32) > 0.5 * MARK)
        block = jnp.concatenate([rows, jnp.where(bad, MASKED, 0.0).astype(BF)], 0)
        kk[w, 3] = block
        turn_keys(w, 3, block)
    pass_on(1)
    score(2)

    halos_arrive(1, vx, jnp.zeros((2, FEAT, WIN), BF))
    for w in range(4):
        for s in range(2):
            block = vx[beside_slot(w, s)]
            vv[w, 1 + s] = block
            turn_values(w, 1 + s, block)
    weigh(1)
    keep_prob(1)
    handed(1)
    for w in range(4):
        block = listed(1, w)
        vv[w, 3] = block
        turn_values(w, 3, block)
    weigh(2)

    for w, p in every:
        keep = GRP * cnt_ref[w // 2, w % 2]
        tops = [m_s[w, p, i, 0:1, :] for i in range(3)]
        top = jnp.maximum(jnp.maximum(tops[0], tops[1]), tops[2])
        shares = [jnp.exp2((t - top) * EXPC) for t in tops]
        total = sum(share * a_s[w, p, i] for i, share in enumerate(shares))
        inverse = 1.0 / total[64:65]
        first = total[:32, :WIN] * inverse[:, :WIN]
        second = total[32:64, WIN:] * inverse[:, WIN:]
        both = jnp.concatenate([first, second], 0)
        product = both * gm[w, 64 * p : 64 * p + 64, :].astype(F32)
        centre = jnp.concatenate(
            [
                jnp.sum(product[:32], axis=0, keepdims=True),
                jnp.sum(product[32:], axis=0, keepdims=True),
            ],
            1,
        )
        c_s[w, p] = jnp.broadcast_to(centre, (8, 256))
        for i, share in enumerate(shares):
            f_s[w, p, i] = jnp.broadcast_to(share * inverse, (8, 256))
        both = jnp.where(iota((64, WIN), 1) < keep, both, 0.0)
        att[w, 64 * p : 64 * p + 64, :] = both.astype(BF)

    def scaled_heads(ref, w, p, factor):
        return diagonal(
            (head(ref, w, 2 * p).astype(F32) * factor[:, :WIN]).astype(BF),
            (head(ref, w, 2 * p + 1).astype(F32) * factor[:, WIN:]).astype(BF),
        )

    def value_terms(part):
        at = span(part)
        for w, p in every:
            rows = scaled_heads(gm, w, p, f_s[w, p, part, 0:1, :])
            g_s[w, FEAT + 64 * p : FEAT + 64 * p + 64, at] = dot_nt(rows, e_s[w, p, at, :])

    def key_terms(part):
        at = span(part)
        for w in range(4):
            slopes, backs, terms = [], [], []
            lows = [e_s[w, p, at, :] for p in range(PAIRS)]
            olds = [gq_s[w, 64 * p : 64 * p + 64, :] for p in range(PAIRS)]
            for p in range(PAIRS):
                prob = grad_prob(w, p, at) if part == 2 else prob_s[w, p, at, :]
                slopes.append((lows[p].astype(F32) * (prob - c_s[w, p, 0:1, :])).astype(BF))
            for p in range(PAIRS):
                scaled = f_s[w, p, part, 0:1, :] * SCALE
                back = dot(rows_of(kk, w, part, p), slopes[p]) * scaled
                backs.append(jnp.concatenate([back[:32, :WIN], back[32:, WIN:]], 0))
                terms.append(dot_nt(scaled_heads(q_ref, w, p, scaled), slopes[p]))
            for p in range(PAIRS):
                rows = slice(64 * p, 64 * p + 64)
                back = backs[p] if part == 1 else backs[p] + olds[p]
                if part == 0:
                    gq_ref[w, rows, :] = back.astype(BF)
                else:
                    gq_s[w, rows, :] = back
                g_s[w, rows, at] = terms[p]

    entries = 32 * n_y
    chosen = []
    for w in range(4):
        row, lane = iota((entries, WIN), 0), iota((entries, WIN), 1)
        want = jnp.zeros((entries, WIN), jnp.int32)
        for f in range(4):
            code = far_ref[w // 2, w % 2, f]
            want = jnp.where(lane // 32 == f, 32 * code + lane - 32 * f, want)
        chosen.append(jnp.where(row == want, 1.0, 0.0).astype(BF))

    def half_copy(which):
        return remote(
            pg_out.at[which, :, 1 - core], pg_half.at[which], half_send, half_recv, which, which, sibling
        )

    def send_half(which):
        spread = None
        for w in range(4):
            term = dot_nt(chosen[w], g_s[w, FEAT * which : FEAT * which + FEAT, 3 * WIN :].astype(BF))
            spread = term if spread is None else spread + term
        spread = pack(spread.reshape(n_y, 32, FEAT)).astype(BF)
        pg_out[which] = spread.reshape(n_z, 2, 48, WIN)
        half_copy(which).start()

    def pg_copy(which, i, src, dst, where):
        i, j = n_z * which + i, n_z * which + dst
        return remote(pg_sum.at[which, src], pg_in.at[which, dst], pg_send, pg_recv, i, j, where)

    def pg_sends(which):
        return [
            pg_copy(which, i, chip_at(step), z, {"sy": 2 * chip_at(step) + core})
            for i, step in enumerate(steps)
        ]

    def send_owners(which):
        half_copy(which).wait_recv()
        both = pg_out[which, :, core].astype(F32) + pg_half[which].astype(F32)
        pg_sum[which] = both.astype(BF)
        start_all(pg_sends(which))

    def toward(w, code, which):
        r, c = divmod(w, 2)
        total = None
        for s in range(2):
            here = (adj_ref[r, c, s] == code).astype(F32)
            term = g_s[w, FEAT * which : FEAT * which + FEAT, (1 + s) * WIN : (2 + s) * WIN] * here
            total = term if total is None else total + term
        return total

    def rims(which):
        def rim(src, dst, i, where):
            rows = pl.ds(FEAT * which, FEAT)
            i = 4 * which + i
            return remote(
                rim_out.at[pl.ds(src, 2), rows],
                rim_in.at[pl.ds(dst, 2), rows],
                rim_send,
                rim_recv,
                i,
                i,
                where,
            )

        return (
            (up, rim(0, 2, 0, x_lo)),
            (down, rim(2, 0, 1, x_hi)),
            (left, rim(4, 6, 2, y_lo)),
            (right, rim(6, 4, 3, y_hi)),
        )

    def send_rims(which):
        at = slice(FEAT * which, FEAT * which + FEAT)
        for w in range(4):
            r, c = divmod(w, 2)
            rim_out[2 * r + c, at] = toward(w, r, which).astype(BF)
            rim_out[4 + 2 * c + r, at] = toward(w, 2 + c, which).astype(BF)
        for there, copy in rims(which):
            pl.when(there)(copy.start)

    mine = pl.ds(pl.multiple_of(hd * FEAT, FEAT), FEAT)
    theirs = pl.ds(pl.multiple_of((1 - hd) * FEAT, FEAT), FEAT)
    for w in range(4):
        bo_out[w] = dot(owt[theirs, :], att[w]).astype(BF)
    share = remote(bo_out, bo_in, bo_send, bo_recv, 0, 0, partner)
    share.start()

    value_terms(2)
    send_half(1)
    value_terms(1)
    send_rims(1)
    key_terms(1)
    send_rims(0)
    send_owners(1)
    key_terms(2)
    send_half(0)
    value_terms(0)
    send_owners(0)
    key_terms(0)

    writes = [
        pltpu.make_async_copy(src, dst, out_sem.at[i])
        for i, (src, dst) in enumerate(
            ((gq_ref, gq_out_ref), (bo_ref, bo_out_ref), (gk_ref, gk_out_ref), (gv_ref, gv_out_ref))
        )
    ]
    writes[0].start()

    for w in range(4):
        bo_own[w] = dot(owt[mine, :], att[w])

    share.wait_recv()
    for w in range(4):
        bo_ref[w] = (bo_own[w] + bo_in[w].astype(F32)).astype(BF)
    writes[1].start()

    for which in (1, 0):
        at = slice(FEAT * which, FEAT * which + FEAT)
        for there, i, slot in ((up, 1, 0), (down, 0, 2), (left, 3, 4), (right, 2, 6)):

            def none(slot=slot, at=at):
                rim_in[slot : slot + 2, at] = jnp.zeros((2, FEAT, WIN), BF)

            pl.when(there)(rims(which)[i][1].wait_recv)
            pl.when(jnp.logical_not(there))(none)

        for step in steps:
            pg_copy(which, 0, chip_at(step), chip_at(step), sibling).wait_recv()
        coarse = pg_sum[which, z].astype(F32)
        for step in steps:
            coarse = coarse + pg_in[which, chip_at(step)].astype(F32)
        coarse = (unpack(coarse) * (1.0 / GRP)).T.astype(BF)
        for w in range(4):
            r, c = divmod(w, 2)
            total = g_s[w, at, :WIN] + toward(w ^ 2, r, which) + toward(w ^ 1, 2 + c, which)
            total = total + rim_in[2 * r + c, at].astype(F32)
            total = total + rim_in[4 + 2 * c + r, at].astype(F32)
            row, lane = iota((32, WIN), 0), iota((32, WIN), 1)
            member = jnp.where(row == 8 * w + lane // GRP, 1.0, 0.0).astype(BF)
            total = total + dot(coarse, member)
            (gv_ref if which else gk_ref)[w] = total.astype(BF)
        writes[2 + which].start()

    for which in range(2):
        for there, copies in halos[which]:
            pl.when(there)(lambda copies=copies: wait_sends(copies))
        wait_sends(started[which])
        half_copy(which).wait_send()
        wait_sends(pg_sends(which))
        for there, copy in rims(which):
            pl.when(there)(copy.wait_send)
    share.wait_send()
    for copy in writes:
        copy.wait()


def hand_over(*refs):
    given, out, held, sems = refs[:4], refs[4:8], refs[8:12], refs[12]
    reads = [pltpu.make_async_copy(given[i], held[i], sems.at[i]) for i in range(4)]
    writes = [pltpu.make_async_copy(held[i], out[i], sems.at[4 + i]) for i in range(4)]
    for copy in reads:
        copy.start()
    for read, write in zip(reads, writes):
        read.wait()
        write.start()
    for copy in writes:
        copy.wait()


def local(n_x, n_y, queries, key_field, value_field, grad_output, out_weight, counts, adjacent, far_list):
    def flat(x):
        return x.reshape(4, -1, WIN)

    hbm = pl.BlockSpec(memory_space=pl.ANY)
    shape = jax.ShapeDtypeStruct((4, FEAT, WIN), BF)
    dma = pltpu.SemaphoreType.DMA
    outs = pl.pallas_call(
        lambda *refs: kernel(n_x, n_y, *refs),
        out_shape=[shape] * 4,
        in_specs=[hbm] * 8,
        out_specs=[hbm] * 4,
        scratch_shapes=[
            pltpu.SMEM(counts.shape, jnp.int32),
            pltpu.SMEM(adjacent.shape, jnp.int32),
            pltpu.SMEM(far_list.shape, jnp.int32),
            pltpu.VMEM((4, FEAT, WIN), BF),
            pltpu.VMEM((4, 2 * FEAT, WIN), BF),
            pltpu.VMEM((FEAT, 2 * FEAT), BF),
            pltpu.VMEM((4, FEAT, WIN), BF),
            pltpu.VMEM((4, FEAT, WIN), BF),
            pltpu.VMEM((4, FEAT, WIN), BF),
            pltpu.VMEM((4, FEAT, WIN), BF),
            pltpu.VMEM((12, AUG, WIN), BF),
            pltpu.VMEM((12, FEAT, WIN), BF),
            pltpu.VMEM((4, 4, AUG, WIN), BF),
            pltpu.VMEM((4, 4, FEAT, WIN), BF),
            pltpu.VMEM((4, PAIRS, 512, WIN), BF),
            pltpu.VMEM((4, 2, 512, WIN), BF),
            pltpu.VMEM((n_y // 2, 2, 48, WIN), BF),
            pltpu.VMEM((n_y // 2, 2, 48, WIN), BF),
            pltpu.VMEM((4, FEAT, WIN), BF),
            pltpu.VMEM((2 * FEAT, FEAT), BF),
            pltpu.VMEM((4, PAIRS, 512, 256), BF),
            pltpu.VMEM((4, PAIRS, 384, 256), F32),
            pltpu.VMEM((4, PAIRS, 3, 8, 256), F32),
            pltpu.VMEM((4, PAIRS, 3, 80, 256), F32),
            pltpu.VMEM((4, PAIRS, 3, 8, 256), F32),
            pltpu.VMEM((4, PAIRS, 8, 256), F32),
            pltpu.VMEM((4, FEAT, WIN), BF),
            pltpu.VMEM((4, FEAT, WIN), F32),
            pltpu.VMEM((4, 2 * FEAT, 512), F32),
            pltpu.VMEM((2, n_y // 2, 2, 48, WIN), BF),
            pltpu.VMEM((2, n_y // 2, 48, WIN), BF),
            pltpu.VMEM((2, n_y // 2, 48, WIN), BF),
            pltpu.VMEM((2, n_y // 2, 48, WIN), BF),
            pltpu.VMEM((8, 2 * FEAT, WIN), BF),
            pltpu.VMEM((8, 2 * FEAT, WIN), BF),
            pltpu.VMEM((4, FEAT, WIN), BF),
            pltpu.VMEM((4, FEAT, WIN), BF),
            pltpu.VMEM((4, FEAT, WIN), F32),
            dma((12,)),
            dma((12,)),
            dma((2 * n_y,)),
            dma((2 * n_y,)),
            dma((8,)),
            dma((8,)),
            dma((n_y,)),
            dma((n_y,)),
            dma((2,)),
            dma((2,)),
            dma((1,)),
            dma((1,)),
            dma((8,)),
            dma((4,)),
        ],
        compiler_params=pltpu.CompilerParams(
            collective_id=0, has_side_effects=True, vmem_limit_bytes=VMEM
        ),
    )(flat(queries), flat(key_field), flat(value_field), flat(grad_output), out_weight, counts, adjacent, far_list)
    block_out, grad_queries, grad_keys, grad_values = pl.pallas_call(
        hand_over,
        out_shape=[shape] * 4,
        in_specs=[hbm] * 4,
        out_specs=[hbm] * 4,
        scratch_shapes=[pltpu.VMEM((4, FEAT, WIN), BF)] * 4 + [dma((8,))],
        compiler_params=pltpu.CompilerParams(vmem_limit_bytes=VMEM),
    )(*outs)
    return (
        block_out.reshape(2, 2, FEAT, WIN),
        grad_queries.reshape(queries.shape),
        grad_keys.reshape(queries.shape),
        grad_values.reshape(queries.shape),
    )


def solution(mesh):
    n_x, n_y = mesh.shape["sx"], mesh.shape["sy"]
    grid = P("sx", "sy")
    heads = P("sx", "sy", "hd", None, None)
    return jax.shard_map(
        lambda *args: local(n_x, n_y, *args),
        mesh=mesh,
        in_specs=(heads, heads, heads, grid, P("hd", None), grid, grid, grid),
        out_specs=(P("sx", "sy", "hd", None), heads, heads, heads),
        check_vma=False,
    )
```
